512 devices in a mesh: region: 16 (over z, core), grp: 32 (over x, y).
Axes of the slice: x: 4, y: 8, z: 8, core: 2. Of those that a mesh axis runs over, the one named last changes fastest.
Arguments:
- ensemble: bfloat16 [256, 1024, 512], P('region', 'grp'), may hold values from -6 to 6
- obs_value: bfloat16 [1024, 512], P('grp'), may hold values from -8 to 8
- obs_prec: bfloat16 [1024, 512], P('grp'), may hold values from 0.25 to 4
- obs_index: int32 [32, 16, 256], P('grp', 'region'), may hold values from 0 to 4095, as said below
- obs_count: int32 [32, 16], P('grp', 'region'), may hold values from 0 to 256
Outputs:
- analysis: bfloat16 [256, 1024, 512], P('region', 'grp')
The draws below stay inside these ranges and needn't reach their ends.
Inputs may be any that keep to these rules, and one draw needn't show every extreme that they name: `obs_index`: the first obs_count entries of a tile name distinct cells of its window, numbered row by row over 64 columns; the later entries are other window cells.
All inputs are finite; a program needn't handle non-finite values.
Results may differ from the reference program's by a relative error of at most 0.0058.
Values may be sent and summed in bfloat16 or wider, within the bound.
A program may use at most 64 MiB of HBM per device.

```python
import math
import jax
import jax.numpy as jnp
from jax import lax

K = 256
TILE = 32
P_SIZE = 256
ITERS = 5
NY = 1024
NX = 512


def observed_tables(key):
    level_key, cell_key, order_key, choose_key = jax.random.split(key, 4)
    tiles_y = NY // TILE
    tiles_x = NX // TILE
    border = TILE // 2
    window = 2 * TILE
    levels = jax.random.randint(level_key, (tiles_y // 4, tiles_x // 4), 1, 8, dtype=jnp.int32)
    chosen = jax.random.randint(choose_key, (), 0, levels.size, dtype=jnp.int32)
    block_ids = jnp.arange(levels.size, dtype=jnp.int32).reshape(levels.shape)
    levels = jnp.where(block_ids == chosen, 1, levels)
    limits = jnp.right_shift(jnp.int32(1 << 20), levels)
    limits = jnp.repeat(jnp.repeat(limits, 4 * TILE, 0), 4 * TILE, 1)
    observed = (jax.random.randint(cell_key, (NY, NX), 0, 1 << 20, dtype=jnp.int32) < limits).astype(jnp.int32)
    observed = jnp.pad(observed, border)
    tile_ids = jnp.arange(tiles_y * tiles_x, dtype=jnp.int32)
    order_keys = jax.random.split(order_key, tiles_y * tiles_x)

    def one_tile(tile_id, tile_key):
        row_start = tile_id // tiles_x * TILE
        col_start = tile_id % tiles_x * TILE
        window_seen = lax.dynamic_slice(observed, (row_start, col_start), (window, window)).reshape(window * window)
        ranking = jax.random.permutation(tile_key, window * window).astype(jnp.int32)
        arranged = jnp.argsort((1 - window_seen) * (window * window) + ranking, stable=True)
        return (arranged[:P_SIZE].astype(jnp.int32), jnp.minimum(jnp.sum(window_seen), P_SIZE).astype(jnp.int32))
    slot_table, counts = jax.vmap(one_tile)(tile_ids, order_keys)
    return (slot_table.reshape(tiles_y, tiles_x, P_SIZE), counts.reshape(tiles_y, tiles_x))


def draw_obs_index(key, part):
    return observed_tables(key)[0]


def draw_obs_count(key, part):
    return observed_tables(key)[1]


def level_of(stream_key, extent, shards, least, high):
    def one(axis_at, blocks):
        heights = jax.random.uniform(jax.random.fold_in(jax.random.fold_in(stream_key, 6), axis_at), (blocks,), jnp.float32, least / len(shards), high / len(shards))
        return jnp.repeat(jnp.exp(heights), extent[axis_at] // blocks).reshape((-1,) + (1,) * (len(extent) - axis_at - 1))

    level = one(*shards[0])
    for cut in shards[1:]:
        level = level * one(*cut)
    return level


def normal_values(stream_key, dims, scale, reach, cuts=(), held_as=jnp.bfloat16):
    result = scale * jax.random.normal(stream_key, dims, jnp.float32)
    if cuts:
        result = result * level_of(stream_key, dims, cuts, -0.22, 0.18)
    return jnp.clip(result, -reach, reach).astype(held_as)


def setup_inputs(seed: int = 0) -> dict:
    seeds = jax.random.split(jax.random.key(seed), 6)
    return {
        "ensemble": normal_values(seeds[0], (K, NY, NX), 1.0, 6.0, ((0, 16), (1, 32))),
        "obs_value": normal_values(seeds[1], (NY, NX), 1.5, 8.0, ((0, 32),)),
        "obs_prec": jnp.clip(jnp.exp(math.log(4.0) - 2.7725887 * jax.random.uniform(seeds[2], (NY, NX), jnp.float32) ** level_of(seeds[2], (NY, NX), ((0, 32),), -0.2, 0.2)), 0.25, 4.0).astype(jnp.bfloat16),
        "obs_index": draw_obs_index(jax.random.fold_in(seeds[5], 71), 0),
        "obs_count": draw_obs_count(jax.random.fold_in(seeds[5], 71), 0),
    }


def inflation_coefficient(slot_cells, tile_cells):
    window = 2 * tile_cells
    centre = tile_cells - 0.5
    offset_y = (slot_cells // window).astype(jnp.float32) - centre
    offset_x = (slot_cells % window).astype(jnp.float32) - centre
    length = 0.375 * tile_cells
    return jnp.exp(-(offset_y * offset_y + offset_x * offset_x) / (2.0 * length * length))

def tile_weights(obs_pert, innovation, weight):
    sample_states = obs_pert.shape[1]
    highest = lax.Precision.HIGHEST
    scaled_product = (obs_pert.astype(jnp.float32) * weight[:, None]).astype(jnp.bfloat16)
    gram_matrix = jnp.dot(scaled_product.T, obs_pert, preferred_element_type=jnp.float32)
    identity = jnp.eye(sample_states, dtype=jnp.float32)
    system = (sample_states - 1.0) * identity + gram_matrix
    frobenius = jnp.sqrt(jnp.sum(system * system))
    matrix_square_root = system / frobenius
    inverse_root = identity
    for number in range(ITERS):
        weight_factor_matrix = 1.5 * identity - 0.5 * jnp.dot(inverse_root, matrix_square_root, precision=highest)
        matrix_square_root = jnp.dot(matrix_square_root, weight_factor_matrix, precision=highest)
        inverse_root = jnp.dot(weight_factor_matrix, inverse_root, precision=highest)
    covariance = jnp.dot(inverse_root, inverse_root, precision=highest) / frobenius
    projected = jnp.dot(innovation * weight, obs_pert.astype(jnp.float32), precision=highest)
    mean_weight = jnp.dot(covariance, projected, precision=highest)
    spread = math.sqrt(sample_states - 1.0) / jnp.sqrt(frobenius)
    return (spread * inverse_root + mean_weight[:, None]).astype(jnp.bfloat16)

def reference(ensemble, obs_value, obs_prec, obs_index, obs_count):
    sample_states, grid_rows, column_total_grid = ensemble.shape
    border = TILE // 2
    window = 2 * TILE
    padded = jnp.pad(ensemble, ((0, 0), (border, border), (border, border)))
    sample_average_state = lax.optimization_barrier(jnp.sum(padded, 0, dtype=jnp.float32)) / sample_states
    sample_anomaly_vector = (padded.astype(jnp.float32) - sample_average_state).astype(jnp.bfloat16)
    values = jnp.pad(obs_value, border)
    precision_field = jnp.pad(obs_prec, border)
    padded_cols = column_total_grid + 2 * border
    tiles_x = column_total_grid // TILE
    slot_ids = jnp.arange(obs_index.shape[2], dtype=jnp.int32)
    column_base = jnp.arange(tiles_x, dtype=jnp.int32) * TILE

    def tile_row(row_id):
        row_start = row_id * TILE
        band_anomaly = lax.dynamic_slice_in_dim(sample_anomaly_vector, row_start, window, 1).reshape(sample_states, window * padded_cols)
        band_average = lax.dynamic_slice_in_dim(sample_average_state, row_start, window, 0).reshape(window * padded_cols)
        band_values = lax.dynamic_slice_in_dim(values, row_start, window, 0).reshape(window * padded_cols)
        band_precision = lax.dynamic_slice_in_dim(precision_field, row_start, window, 0).reshape(window * padded_cols)
        slot_cells = lax.dynamic_index_in_dim(obs_index, row_id, 0, keepdims=False)
        counts = lax.dynamic_index_in_dim(obs_count, row_id, 0, keepdims=False)
        located = slot_cells // window * padded_cols + column_base[:, None] + slot_cells % window
        obs_pert = jnp.take(band_anomaly, located, axis=1)
        innovation = jnp.take(band_values, located).astype(jnp.float32) - jnp.take(band_average, located)
        live_slot = slot_ids[None, :] < counts[:, None]
        weight = jnp.where(live_slot, jnp.take(band_precision, located).astype(jnp.float32) * inflation_coefficient(slot_cells, TILE), jnp.float32(0.0))
        weights = jax.vmap(tile_weights)(jnp.transpose(obs_pert, (1, 2, 0)), innovation, weight)
        interior = lax.dynamic_slice_in_dim(sample_anomaly_vector, row_start + border, TILE, 1)[:, :, border:border + column_total_grid]
        interior = interior.reshape(sample_states, TILE, tiles_x, TILE)
        interior_average = lax.dynamic_slice_in_dim(sample_average_state, row_start + border, TILE, 0)[:, border:border + column_total_grid]
        interior_average = interior_average.reshape(TILE, tiles_x, TILE)
        update = jnp.einsum('iaxb,xik->kaxb', interior.astype(jnp.float32), weights.astype(jnp.float32))
        return (update + interior_average).astype(jnp.bfloat16).reshape(sample_states, TILE, column_total_grid)
    rows_out = lax.map(tile_row, jnp.arange(grid_rows // TILE, dtype=jnp.int32))
    return jnp.transpose(rows_out, (1, 0, 2, 3)).reshape(sample_states, grid_rows, column_total_grid)
```

```python
import functools
import math

import jax
import jax.numpy as jnp
from jax import lax
from jax.experimental import pallas as pl
from jax.experimental.pallas import tpu as pltpu
from jax.sharding import PartitionSpec as P

TILE = 32
ITERS = 5
LANES = 128
MESH = pl.DeviceIdType.MESH
F32 = jnp.float32
BF16 = jnp.bfloat16


def swap_blocks(parts):
    lane = lax.broadcasted_iota(jnp.int32, parts[0].shape, 1)
    low = lane < 64
    even = (lane // 32) % 2 == 0
    half = []
    for a, b in ((parts[0], parts[2]), (parts[1], parts[3])):
        half.append(
            (
                jnp.where(low, a, pltpu.roll(b, 64, 1)),
                jnp.where(low, pltpu.roll(a, 64, 1), b),
            )
        )
    result = []
    for which in range(2):
        a, b = half[0][which], half[1][which]
        result.append(jnp.where(even, a, pltpu.roll(b, 32, 1)))
        result.append(jnp.where(even, pltpu.roll(a, 96, 1), b))
    return result


def split(a):
    high = a.astype(BF16)
    return high, (a - high.astype(F32)).astype(BF16)


def product(a, b):
    return (
        jnp.dot(a[0], b[0], preferred_element_type=F32)
        + jnp.dot(a[0], b[1], preferred_element_type=F32)
        + jnp.dot(a[1], b[0], preferred_element_type=F32)
    )


def window_base(tile):
    return jnp.clip((tile * TILE + LANES - TILE // 2) // LANES - 1, 0, 2)


def column_select(cells, tile):
    base = window_base(tile)
    column = cells % (2 * TILE) + (tile * TILE - TILE // 2 - base * LANES)
    place = lax.broadcasted_iota(jnp.int32, (2 * LANES, cells.shape[1]), 0)
    return jnp.where(place == column, F32(1.0), F32(0.0)).astype(BF16)


def row_select(columns, rows, members):
    slots = columns.shape[1]
    parts = columns.reshape(members, 4, 8, slots)
    place = lax.broadcasted_iota(jnp.int32, (8, slots), 0)
    chosen = jnp.zeros((members, 8, slots), F32)
    for q in range(4):
        mask = jnp.broadcast_to((place + 8 * q == rows)[None], chosen.shape)
        chosen = jnp.where(mask, parts[:, q], chosen)
    return chosen.reshape(members * 8, slots)


def own_rows(cells):
    return cells // (2 * TILE) - TILE // 2


def halo_rows(cells, first, last):
    row = cells // (2 * TILE)
    above = jnp.where(first, -1, row)
    below = jnp.where(last, -1, row - TILE)
    return jnp.where(row < TILE // 2, above, jnp.where(row >= 3 * TILE // 2, below, -1))


def kernel(
    regions,
    bands,
    ens,
    value,
    precision,
    index,
    count,
    out,
    held,
    halo,
    planes,
    cells_all,
    shuffle,
    main_send,
    main_recv,
    selected,
    obs_send,
    obs_recv,
    back_send,
    back_recv,
    result,
    load_sem,
    halo_sems,
    plane_sems,
    cell_sems,
    main_sems,
    obs_sems,
    back_sems,
    out_sems,
):
    r = lax.axis_index("region")
    g = lax.axis_index("grp")
    up = lax.rem(g + bands - 1, bands)
    down = lax.rem(g + 1, bands)
    members = ens.shape[0]
    total = members * regions
    half = TILE // 2
    slots = index.shape[2]
    groups = regions // 4

    def peer(d):
        return lax.rem(r + d, regions)

    barrier = pltpu.get_barrier_semaphore()

    def greet(d, carry):
        pl.semaphore_signal(barrier, inc=1, device_id={"region": peer(d)}, device_id_type=MESH)
        return carry

    load = pltpu.make_async_copy(ens, held, load_sem)
    load.start()
    for band in (up, down):
        pl.semaphore_signal(barrier, inc=1, device_id={"grp": band}, device_id_type=MESH)
    lax.fori_loop(1, regions, greet, 0)
    cells_all[r] = index[0]
    load.wait()
    pl.semaphore_wait(barrier, regions + 1)

    base_lanes = pl.ds(pl.multiple_of(window_base(r) * LANES, LANES), 2 * LANES)

    def halo_copy(side):
        band = (down, up)[side]
        rows = (pl.ds(half, half), pl.ds(0, half))[side]
        place = pl.ds(side * half, half)
        pairs = [(held.at[:, rows, :], halo.at[:, place, :], halo_sems, side)]
        for n, plane in enumerate((value, precision)):
            pairs.append((plane.at[rows, base_lanes], planes.at[n, place, :], plane_sems, 2 * n + side))
        return [
            pltpu.make_async_remote_copy(
                src_ref=src,
                dst_ref=dst,
                send_sem=sems.at[0, at],
                recv_sem=sems.at[1, at],
                device_id={"grp": band},
                device_id_type=MESH,
            )
            for src, dst, sems, at in pairs
        ]

    def cell_copy(to, slot):
        return pltpu.make_async_remote_copy(
            src_ref=cells_all.at[r],
            dst_ref=cells_all.at[slot],
            send_sem=cell_sems.at[0, to],
            recv_sem=cell_sems.at[1, slot],
            device_id={"region": to},
            device_id_type=MESH,
        )

    def block_copy(send, recv, sems, to, slot):
        return pltpu.make_async_remote_copy(
            src_ref=send.at[to],
            dst_ref=recv.at[slot],
            send_sem=sems.at[0, to],
            recv_sem=sems.at[1, slot],
            device_id={"region": to},
            device_id_type=MESH,
        )

    def send_cells(d, carry):
        cell_copy(peer(d), r).start()
        return carry

    lax.fori_loop(1, regions, send_cells, 0)
    halo_copies = halo_copy(0) + halo_copy(1)
    for copy in halo_copies:
        copy.start()

    def pack_group(step, carry):
        group = lax.rem(r // 4 + step, groups)
        lanes = pl.ds(pl.multiple_of(group * LANES, LANES), LANES)

        def pack_member(m, inner):
            block = held[m, :, lanes].astype(F32)
            parts = swap_blocks([block[8 * q : 8 * q + 8] for q in range(4)])
            at = pl.ds(pl.multiple_of(m * 8, 8), 8)
            for t in range(4):
                shuffle[t, at, :] = parts[t]
            return inner

        lax.fori_loop(0, members, pack_member, 0)

        for t in range(4):
            tile = 4 * group + t
            for s in range(8):
                main_send[tile, :, s * LANES : (s + 1) * LANES] = shuffle[
                    t, pl.ds(s, members, stride=8), :
                ].astype(BF16)

            @pl.when(tile != r)
            def _():
                block_copy(main_send, main_recv, main_sems, tile, r).start()

            @pl.when(tile == r)
            def _():
                main_recv[r] = main_send[r]

        return carry

    lax.fori_loop(0, groups, pack_group, 0)

    gather_rows = lax.broadcasted_iota(jnp.int32, (members, members * 8), 0)
    gather_cols = lax.broadcasted_iota(jnp.int32, (members, members * 8), 1)
    fold = jnp.where(gather_cols // 8 == gather_rows, F32(1.0), F32(0.0)).astype(BF16)

    def choose(source, cells, rows, tile):
        lanes = pl.ds(pl.multiple_of(window_base(tile) * LANES, LANES), 2 * LANES)
        columns = jnp.dot(
            source[:, :, lanes].reshape(members * TILE, 2 * LANES),
            column_select(cells, tile),
            preferred_element_type=F32,
        )
        picked = row_select(columns, rows, members).astype(BF16)
        return jnp.dot(fold, picked, preferred_element_type=F32)

    def from_own(d, carry):
        tile = peer(d)

        @pl.when(tile != r)
        def _():
            cell_copy(tile, tile).wait_recv()

        cells = cells_all[tile]
        selected[tile] = choose(held, cells, own_rows(cells), tile)
        return carry

    lax.fori_loop(0, regions, from_own, 0)

    for copy in halo_copies:
        copy.wait_recv()

    def from_halo(d, carry):
        tile = peer(d)
        cells = cells_all[tile]
        rows = halo_rows(cells, g == 0, g == bands - 1)
        obs_send[tile] = (selected[tile] + choose(halo, cells, rows, tile)).astype(BF16)
        block_copy(obs_send, obs_recv, obs_sems, tile, r).start()
        return carry

    lax.fori_loop(1, regions, from_halo, 0)
    cells = cells_all[r]
    rows_own = own_rows(cells)
    rows_halo = halo_rows(cells, g == 0, g == bands - 1)
    obs_recv[r] = (selected[r] + choose(halo, cells, rows_halo, r)).astype(BF16)

    fields = jnp.concatenate(
        [value[:, base_lanes], planes[0], precision[:, base_lanes], planes[1]], axis=0
    )
    columns = jnp.dot(fields, column_select(cells, r), preferred_element_type=F32)
    place = lax.broadcasted_iota(jnp.int32, (TILE, slots), 0)
    at_own = place == rows_own
    at_halo = place == rows_halo

    def field(n):
        own = jnp.where(at_own, columns[2 * n * TILE : (2 * n + 1) * TILE], F32(0.0))
        beside = jnp.where(at_halo, columns[(2 * n + 1) * TILE : (2 * n + 2) * TILE], F32(0.0))
        return jnp.sum(own + beside, axis=0, keepdims=True)

    values_at = field(0)
    precision_at = field(1)
    offset_y = (cells // (2 * TILE)).astype(F32) - (TILE - 0.5)
    offset_x = (cells % (2 * TILE)).astype(F32) - (TILE - 0.5)
    length = 0.375 * TILE
    inflation = jnp.exp(-(offset_y * offset_y + offset_x * offset_x) / (2.0 * length * length))
    live = lax.broadcasted_iota(jnp.int32, (1, slots), 1) < count[0, 0]
    weight = jnp.where(live, precision_at * inflation, F32(0.0))

    def wait_block(recv, sems):
        def body(d, carry):
            src = peer(d)
            block_copy(recv, recv, sems, src, src).wait_recv()
            return carry

        lax.fori_loop(1, regions, body, 0)

    wait_block(obs_recv, obs_sems)

    raw = obs_recv[...].reshape(total, slots).astype(F32)
    average = jnp.sum(raw, axis=0, keepdims=True) * (1.0 / total)
    pert = (raw - average).astype(BF16)
    scaled = weight * (values_at - average)
    weighted = (pert.astype(F32) * weight).astype(BF16)
    across = (((1,), (1,)), ((), ()))
    diagonal = lax.broadcasted_iota(jnp.int32, (total, total), 0) == lax.broadcasted_iota(
        jnp.int32, (total, total), 1
    )

    def plus_identity(scale, a):
        return a + jnp.where(diagonal, F32(scale), F32(0.0))

    system = plus_identity(
        total - 1.0, lax.dot_general(pert, weighted, across, preferred_element_type=F32)
    )
    squares = jnp.sum(system * system, axis=0, keepdims=True)
    frobenius = jnp.sqrt(jnp.sum(squares, axis=1, keepdims=True))
    inverse_frobenius = 1.0 / frobenius

    scaled_high = scaled.astype(BF16)
    rest = scaled - scaled_high.astype(F32)
    scaled_mid = rest.astype(BF16)
    scaled_low = (rest - scaled_mid.astype(F32)).astype(BF16)

    def stack(*rows):
        n = rows[0].shape[1]
        place = lax.broadcasted_iota(jnp.int32, (16, n), 0)
        whole = jnp.zeros((16, n), F32)
        for at, row in enumerate(rows):
            whole = jnp.where(place == at, row.astype(F32), whole)
        return whole.astype(BF16)

    projected = jnp.sum(
        lax.dot_general(
            stack(scaled_high, scaled_mid, scaled_low), pert, across, preferred_element_type=F32
        ),
        axis=0,
        keepdims=True,
    )

    start = system * inverse_frobenius
    root = split(start)
    inverse_root = plus_identity(1.5, -0.5 * start)
    factor = split(inverse_root)
    inverse_pair = factor
    root = split(product(root, factor))
    for number in range(1, ITERS):
        factor = split(plus_identity(1.5, -0.5 * product(root, inverse_pair)))
        if number < ITERS - 1:
            root = split(product(factor, root))
        inverse_root = product(inverse_pair, factor)
        inverse_pair = split(inverse_root)

    def row_product(row):
        pair = stack(*split(row))
        first = jnp.dot(pair, inverse_pair[0], preferred_element_type=F32)
        second = jnp.dot(pair, inverse_pair[1], preferred_element_type=F32)
        return first[0:1] + first[1:2] + second[0:1]

    mean_weight = row_product(row_product(projected)) * inverse_frobenius
    spread = math.sqrt(total - 1.0) / jnp.sqrt(frobenius)
    weights = (spread * inverse_root + mean_weight).astype(BF16)

    wait_block(main_recv, main_sems)
    cell_total = main_recv.shape[2]
    step = 2 * LANES
    for n in range(cell_total // step):
        at = slice(n * step, (n + 1) * step)
        prior = main_recv[:, :, at].reshape(total, step).astype(F32)
        mean = jnp.sum(prior, axis=0, keepdims=True) * (1.0 / total)
        update = jnp.dot(weights, (prior - mean).astype(BF16), preferred_element_type=F32)
        back_send[:, :, at] = (update + mean).astype(BF16).reshape(regions, members, step)

    def send_back(d, carry):
        block_copy(back_send, back_recv, back_sems, peer(d), r).start()
        return carry

    lax.fori_loop(1, regions, send_back, 0)
    back_recv[r] = back_send[r]

    def out_copy(group):
        lanes = pl.ds(pl.multiple_of(group * LANES, LANES), LANES)
        return pltpu.make_async_copy(result.at[:, :, lanes], out.at[:, :, lanes], out_sems.at[group])

    def unpack_group(step, carry):
        group = lax.rem(r // 4 + step, groups)
        lanes = pl.ds(pl.multiple_of(group * LANES, LANES), LANES)
        for t in range(4):
            tile = 4 * group + t

            @pl.when(tile != r)
            def _():
                block_copy(back_recv, back_recv, back_sems, tile, tile).wait_recv()

            for s in range(8):
                shuffle[t, pl.ds(s, members, stride=8), :] = back_recv[
                    tile, :, s * LANES : (s + 1) * LANES
                ].astype(F32)

        def unpack_member(m, inner):
            at = pl.ds(pl.multiple_of(m * 8, 8), 8)
            parts = swap_blocks([shuffle[t, at, :] for t in range(4)])
            result[m, :, lanes] = jnp.concatenate(parts, axis=0).astype(BF16)
            return inner

        lax.fori_loop(0, members, unpack_member, 0)
        out_copy(group).start()
        return carry

    lax.fori_loop(0, groups, unpack_group, 0)

    def finish_sends(d, carry):
        to = peer(d)
        cell_copy(to, r).wait_send()
        block_copy(main_send, main_recv, main_sems, to, r).wait_send()
        block_copy(obs_send, obs_recv, obs_sems, to, r).wait_send()
        block_copy(back_send, back_recv, back_sems, to, r).wait_send()
        return carry

    lax.fori_loop(1, regions, finish_sends, 0)
    for copy in halo_copies:
        copy.wait_send()

    def finish_out(group, carry):
        out_copy(group).wait()
        return carry

    lax.fori_loop(0, groups, finish_out, 0)


def solution(mesh):
    regions = mesh.shape["region"]
    bands = mesh.shape["grp"]

    def shards(ensemble, obs_value, obs_prec, obs_index, obs_count):
        members, rows, columns = ensemble.shape
        slots = obs_index.shape[2]
        cells = rows * TILE
        total = members * regions
        vmem = pl.BlockSpec(memory_space=pltpu.VMEM)
        hbm = pl.BlockSpec(memory_space=pl.ANY)
        return pl.pallas_call(
            functools.partial(kernel, regions, bands),
            out_shape=jax.ShapeDtypeStruct(ensemble.shape, BF16),
            in_specs=[hbm, vmem, vmem, vmem, pl.BlockSpec(memory_space=pltpu.SMEM)],
            out_specs=hbm,
            scratch_shapes=[
                pltpu.VMEM((members, rows, columns), BF16),
                pltpu.VMEM((members, rows, columns), BF16),
                pltpu.VMEM((2, rows, 2 * LANES), BF16),
                pltpu.VMEM((regions, 1, slots), jnp.int32),
                pltpu.VMEM((4, members * 8, LANES), F32),
                pltpu.VMEM((regions, members, cells), BF16),
                pltpu.VMEM((regions, members, cells), BF16),
                pltpu.VMEM((regions, members, slots), F32),
                pltpu.VMEM((regions, members, slots), BF16),
                pltpu.VMEM((regions, members, slots), BF16),
                pltpu.VMEM((regions, members, cells), BF16),
                pltpu.VMEM((regions, members, cells), BF16),
                pltpu.VMEM((members, rows, columns), BF16),
                pltpu.SemaphoreType.DMA,
                pltpu.SemaphoreType.DMA((2, 2)),
                pltpu.SemaphoreType.DMA((2, 4)),
                pltpu.SemaphoreType.DMA((2, regions)),
                pltpu.SemaphoreType.DMA((2, regions)),
                pltpu.SemaphoreType.DMA((2, regions)),
                pltpu.SemaphoreType.DMA((2, regions)),
                pltpu.SemaphoreType.DMA((regions // 4,)),
            ],
            compiler_params=pltpu.CompilerParams(
                collective_id=0, has_side_effects=True, vmem_limit_bytes=32 * 1024 * 1024
            ),
        )(ensemble, obs_value, obs_prec, obs_index, obs_count)

    placed = (
        P("region", "grp", None),
        P("grp", None),
        P("grp", None),
        P("grp", "region", None),
        P("grp", "region"),
    )
    return jax.shard_map(
        shards, mesh=mesh, in_specs=placed, out_specs=P("region", "grp", None), check_vma=False
    )
```

```python
import functools
import math

import jax
import jax.numpy as jnp
from jax import lax
from jax.experimental import pallas as pl
from jax.experimental.pallas import tpu as pltpu
from jax.sharding import PartitionSpec as P

TILE = 32
ITERS = 5
LANES = 128
MESH = pl.DeviceIdType.MESH
F32 = jnp.float32
BF16 = jnp.bfloat16


def swap_blocks(parts):
    lane = lax.broadcasted_iota(jnp.int32, parts[0].shape, 1)
    low = lane < 64
    even = (lane // 32) % 2 == 0
    half = []
    for a, b in ((parts[0], parts[2]), (parts[1], parts[3])):
        half.append(
            (
                jnp.where(low, a, pltpu.roll(b, 64, 1)),
                jnp.where(low, pltpu.roll(a, 64, 1), b),
            )
        )
    result = []
    for which in range(2):
        a, b = half[0][which], half[1][which]
        result.append(jnp.where(even, a, pltpu.roll(b, 32, 1)))
        result.append(jnp.where(even, pltpu.roll(a, 96, 1), b))
    return result


def split(a):
    high = a.astype(BF16)
    return high, (a - high.astype(F32)).astype(BF16)


def product(a, b):
    return (
        jnp.dot(a[0], b[0], preferred_element_type=F32)
        + jnp.dot(a[0], b[1], preferred_element_type=F32)
        + jnp.dot(a[1], b[0], preferred_element_type=F32)
    )


def window_base(tile):
    return jnp.clip((tile * TILE + LANES - TILE // 2) // LANES - 1, 0, 2)


def padded_base(tile):
    return (tile * TILE + LANES - TILE // 2) // LANES


def column_select(cells, tile, first):
    column = cells % (2 * TILE) + (tile * TILE - TILE // 2 - first)
    place = lax.broadcasted_iota(jnp.int32, (2 * LANES, cells.shape[1]), 0)
    return jnp.where(place == column, F32(1.0), F32(0.0)).astype(BF16)


def fold_rows(parts):
    place = lax.broadcasted_iota(jnp.int32, parts[0].shape, 0)
    distance = 1
    while len(parts) > 1:
        odd = (place // distance) % 2 == 1
        parts = [
            jnp.where(odd, b, a) + pltpu.roll(jnp.where(odd, a, b), distance, 0)
            for a, b in zip(parts[::2], parts[1::2])
        ]
        distance *= 2
    return parts[0]


def row_select(columns, rows, members):
    slots = columns.shape[1]
    place = lax.broadcasted_iota(jnp.int32, (8, slots), 0)
    masks = [place + 8 * q == rows for q in range(4)]
    chosen = []
    for m in range(members):
        part = jnp.zeros((8, slots), F32)
        for q in range(4):
            at = m * TILE + 8 * q
            part = jnp.where(masks[q], columns[at : at + 8], part)
        chosen.append(part)
    return jnp.concatenate([fold_rows(chosen[m : m + 8]) for m in range(0, members, 8)], axis=0)


def own_rows(cells):
    return cells // (2 * TILE) - TILE // 2


def halo_rows(cells, first, last):
    row = cells // (2 * TILE)
    above = jnp.where(first, -1, row)
    below = jnp.where(last, -1, row - TILE)
    return jnp.where(row < TILE // 2, above, jnp.where(row >= 3 * TILE // 2, below, -1))


def kernel(
    regions,
    bands,
    ens,
    value,
    precision,
    index,
    count,
    out,
    held,
    halo,
    planes,
    planes_halo,
    cells_all,
    live_count,
    shuffle,
    main_send,
    main_recv,
    selected,
    obs_send,
    obs_recv,
    back_send,
    back_recv,
    load_sems,
    halo_sems,
    plane_sems,
    cell_sems,
    main_sems,
    obs_sems,
    back_sems,
):
    r = lax.axis_index("region")
    g = lax.axis_index("grp")
    up = lax.rem(g + bands - 1, bands)
    down = lax.rem(g + 1, bands)
    members = ens.shape[0]
    total = members * regions
    half = TILE // 2
    slots = index.shape[2]
    columns_all = ens.shape[2]
    groups = regions // 4
    chips = regions // 2
    first_group = r // 4
    chip, core = r // 2, lax.rem(r, 2)

    def peer(d):
        return lax.rem(r + d, regions)

    def ring_order(distances):
        return [
            2 * lax.rem(chip + d % chips, chips) + (1 - core if other else core)
            for d in distances
            for other in (0, 1)
            if d % chips or other
        ]

    barrier = pltpu.get_barrier_semaphore()
    for to in ring_order((4, 3, -3, 2, -2, 1, -1, 0)):
        pl.semaphore_signal(barrier, inc=1, device_id={"region": to}, device_id_type=MESH)
    for band in (up, down):
        pl.semaphore_signal(barrier, inc=1, device_id={"grp": band}, device_id_type=MESH)
    base_lanes = pl.ds(pl.multiple_of(window_base(r) * LANES, LANES), 2 * LANES)
    loads = [
        pltpu.make_async_copy(src, dst, load_sems.at[n])
        for n, (src, dst) in enumerate(
            (
                (ens, held.at[:, :, LANES : LANES + columns_all]),
                (value.at[:, base_lanes], planes.at[0]),
                (precision.at[:, base_lanes], planes.at[1]),
                (index.at[0], cells_all.at[r]),
                (count, live_count),
            )
        )
    ]
    for copy in loads:
        copy.start()
    zeros = jnp.zeros((members, TILE, LANES), BF16)
    for side in (slice(0, LANES), slice(LANES + columns_all, 2 * LANES + columns_all)):
        held[:, :, side] = zeros
        halo[:, :, side] = zeros
    loads[0].wait()

    def group_lanes(group):
        return pl.ds(pl.multiple_of(group * LANES, LANES), LANES)

    def padded_lanes(group):
        return group_lanes(group + 1)

    def pack_group(group, carry):
        lanes = padded_lanes(group)
        for m in range(members):
            block = held[m, :, lanes].astype(F32)
            parts = swap_blocks([block[8 * q : 8 * q + 8] for q in range(4)])
            for t in range(4):
                shuffle[t, m * 8 : m * 8 + 8, :] = parts[t]
        for t in range(4):
            for s in range(8):
                main_send[4 * group + t, :, s * LANES : (s + 1) * LANES] = shuffle[
                    t, pl.ds(s, members, stride=8), :
                ].astype(BF16)
        return carry

    lax.fori_loop(0, groups, pack_group, 0)
    for copy in loads[1:]:
        copy.wait()
    main_recv[r] = main_send[r]
    pl.semaphore_wait(barrier, regions + 1)

    def band_copy(src, dst, sems, at, side):
        return pltpu.make_async_remote_copy(
            src_ref=src,
            dst_ref=dst,
            send_sem=sems.at[0, at],
            recv_sem=sems.at[1, at],
            device_id={"grp": (down, up)[side]},
            device_id_type=MESH,
        )

    rows_out = (pl.ds(half, half), pl.ds(0, half))
    rows_in = (pl.ds(0, half), pl.ds(half, half))

    def halo_copies(step):
        group = lax.rem(first_group + step, groups)
        lanes = padded_lanes(group)
        return [
            band_copy(
                held.at[:, rows_out[side], lanes],
                halo.at[:, rows_in[side], lanes],
                halo_sems,
                2 * group + side,
                side,
            )
            for side in range(2)
        ]

    plane_copies = [
        band_copy(
            planes.at[n, rows_out[side], :],
            planes_halo.at[n, rows_in[side], :],
            plane_sems,
            2 * n + side,
            side,
        )
        for n in range(2)
        for side in range(2)
    ]

    def cell_copy(to, slot):
        return pltpu.make_async_remote_copy(
            src_ref=cells_all.at[r],
            dst_ref=cells_all.at[slot],
            send_sem=cell_sems.at[0, to],
            recv_sem=cell_sems.at[1, slot],
            device_id={"region": to},
            device_id_type=MESH,
        )

    def block_copy(send, recv, sems, to, slot):
        return pltpu.make_async_remote_copy(
            src_ref=send.at[to],
            dst_ref=recv.at[slot],
            send_sem=sems.at[0, to],
            recv_sem=sems.at[1, slot],
            device_id={"region": to},
            device_id_type=MESH,
        )

    def send_main(distances):
        for to in ring_order(distances):
            block_copy(main_send, main_recv, main_sems, to, r).start()

    for to in ring_order((4, 3, -3, 2, -2, 1, -1, 0)):
        cell_copy(to, r).start()
    for step in range(groups):
        for copy in halo_copies(step):
            copy.start()
    for copy in plane_copies:
        copy.start()
    send_main((3, -3, 1, -1))

    def choose(source, rows, tile):
        base = padded_base(tile)
        lanes = pl.ds(pl.multiple_of(base * LANES, LANES), 2 * LANES)
        columns = jnp.dot(
            source[:, :, lanes].reshape(members * TILE, 2 * LANES),
            column_select(cells_all[tile], tile, (base - 1) * LANES),
            preferred_element_type=F32,
        )
        return row_select(columns, rows, members)

    def tiles_of(step):
        return [peer_tile(4 * step + n) for n in range(4)]

    def peer_tile(n):
        return lax.rem(4 * first_group + 1 + n, regions)

    def from_own(step, carry):
        tiles = tiles_of(step)
        for tile in tiles:

            @pl.when(tile != r)
            def _():
                cell_copy(tile, tile).wait_recv()

        for tile in tiles:
            selected[tile] = choose(held, own_rows(cells_all[tile]), tile)
        return carry

    lax.fori_loop(0, groups, from_own, 0)

    def from_halo(step, carry):
        @pl.when(step == 0)
        def _():
            for copy in halo_copies(0):
                copy.wait_recv()

        @pl.when(step < groups - 1)
        def _():
            for copy in halo_copies(step + 1):
                copy.wait_recv()

        tiles = tiles_of(step)
        for tile in tiles:
            rows = halo_rows(cells_all[tile], g == 0, g == bands - 1)
            obs_send[tile] = (selected[tile] + choose(halo, rows, tile)).astype(BF16)
        for tile in tiles:

            @pl.when(tile != r)
            def _():
                block_copy(obs_send, obs_recv, obs_sems, tile, r).start()

        return carry

    lax.fori_loop(0, groups, from_halo, 0)
    send_main((4, 2, -2, 0))
    obs_recv[r] = obs_send[r]

    for copy in plane_copies:
        copy.wait_recv()
    cells = cells_all[r]
    fields = jnp.concatenate([planes[0], planes_halo[0], planes[1], planes_halo[1]], axis=0)
    columns = jnp.dot(fields, column_select(cells, r, window_base(r) * LANES), preferred_element_type=F32)
    place = lax.broadcasted_iota(jnp.int32, (TILE, slots), 0)
    at_own = place == own_rows(cells)
    at_halo = place == halo_rows(cells, g == 0, g == bands - 1)

    def field(n):
        own = jnp.where(at_own, columns[2 * n * TILE : (2 * n + 1) * TILE], F32(0.0))
        beside = jnp.where(at_halo, columns[(2 * n + 1) * TILE : (2 * n + 2) * TILE], F32(0.0))
        return jnp.sum(own + beside, axis=0, keepdims=True)

    values_at = field(0)
    precision_at = field(1)
    offset_y = (cells // (2 * TILE)).astype(F32) - (TILE - 0.5)
    offset_x = (cells % (2 * TILE)).astype(F32) - (TILE - 0.5)
    length = 0.375 * TILE
    inflation = jnp.exp(-(offset_y * offset_y + offset_x * offset_x) / (2.0 * length * length))
    live = lax.broadcasted_iota(jnp.int32, (1, slots), 1) < live_count[...]
    weight = jnp.where(live, precision_at * inflation, F32(0.0))

    def wait_block(recv, sems):
        def body(d, carry):
            src = peer(d)
            block_copy(recv, recv, sems, src, src).wait_recv()
            return carry

        lax.fori_loop(1, regions, body, 0)

    wait_block(obs_recv, obs_sems)

    raw = obs_recv[...].reshape(total, slots).astype(F32)
    average = jnp.sum(raw, axis=0, keepdims=True) * (1.0 / total)
    pert = (raw - average).astype(BF16)
    scaled = weight * (values_at - average)
    weighted = (pert.astype(F32) * weight).astype(BF16)
    across = (((1,), (1,)), ((), ()))
    diagonal = lax.broadcasted_iota(jnp.int32, (total, total), 0) == lax.broadcasted_iota(
        jnp.int32, (total, total), 1
    )

    def plus_identity(scale, a):
        return a + jnp.where(diagonal, F32(scale), F32(0.0))

    system = plus_identity(
        total - 1.0, lax.dot_general(pert, weighted, across, preferred_element_type=F32)
    )
    squares = jnp.sum(system * system, axis=0, keepdims=True)
    frobenius = jnp.sqrt(jnp.sum(squares, axis=1, keepdims=True))
    inverse_frobenius = 1.0 / frobenius

    scaled_high = scaled.astype(BF16)
    rest = scaled - scaled_high.astype(F32)
    scaled_mid = rest.astype(BF16)
    scaled_low = (rest - scaled_mid.astype(F32)).astype(BF16)

    def stack(*rows):
        n = rows[0].shape[1]
        place = lax.broadcasted_iota(jnp.int32, (16, n), 0)
        whole = jnp.zeros((16, n), F32)
        for at, row in enumerate(rows):
            whole = jnp.where(place == at, row.astype(F32), whole)
        return whole.astype(BF16)

    projected = jnp.sum(
        lax.dot_general(
            stack(scaled_high, scaled_mid, scaled_low), pert, across, preferred_element_type=F32
        ),
        axis=0,
        keepdims=True,
    )

    start = system * inverse_frobenius
    root = split(start)
    inverse_root = plus_identity(1.5, -0.5 * start)
    factor = split(inverse_root)
    inverse_pair = factor
    root = split(product(root, factor))
    for number in range(1, ITERS):
        factor = split(plus_identity(1.5, -0.5 * product(root, inverse_pair)))
        if number < ITERS - 1:
            root = split(product(factor, root))
        inverse_root = product(inverse_pair, factor)
        inverse_pair = split(inverse_root)

    def row_product(row):
        pair = stack(*split(row))
        first = jnp.dot(pair, inverse_pair[0], preferred_element_type=F32)
        second = jnp.dot(pair, inverse_pair[1], preferred_element_type=F32)
        return first[0:1] + first[1:2] + second[0:1]

    mean_weight = row_product(row_product(projected)) * inverse_frobenius
    spread = math.sqrt(total - 1.0) / jnp.sqrt(frobenius)
    weights = (spread * inverse_root + mean_weight).astype(BF16)

    wait_block(main_recv, main_sems)
    cell_total = main_recv.shape[2]
    step = 2 * LANES
    for n in range(cell_total // step):
        at = slice(n * step, (n + 1) * step)
        prior = main_recv[:, :, at].reshape(total, step).astype(F32)
        mean = jnp.sum(prior, axis=0, keepdims=True) * (1.0 / total)
        update = jnp.dot(weights, (prior - mean).astype(BF16), preferred_element_type=F32)
        back_send[:, :, at] = (update + mean).astype(BF16).reshape(regions, members, step)

    for to in ring_order((4, 3, -3, 2, -2, 1, -1, 0)):
        block_copy(back_send, back_recv, back_sems, to, r).start()
    back_recv[r] = back_send[r]

    def unpack_group(step, carry):
        group = lax.rem(first_group + 2 + step, groups)
        lanes = group_lanes(group)
        for t in range(4):
            tile = 4 * group + t

            @pl.when(tile != r)
            def _():
                block_copy(back_recv, back_recv, back_sems, tile, tile).wait_recv()

        for t in range(4):
            for s in range(8):
                shuffle[t, pl.ds(s, members, stride=8), :] = back_recv[
                    4 * group + t, :, s * LANES : (s + 1) * LANES
                ].astype(F32)
        for m in range(members):
            parts = swap_blocks([shuffle[t, m * 8 : m * 8 + 8, :] for t in range(4)])
            out[m, :, lanes] = jnp.concatenate(parts, axis=0).astype(BF16)
        return carry

    lax.fori_loop(0, groups, unpack_group, 0)

    def finish_sends(d, carry):
        to = peer(d)
        cell_copy(to, r).wait_send()
        block_copy(main_send, main_recv, main_sems, to, r).wait_send()
        block_copy(obs_send, obs_recv, obs_sems, to, r).wait_send()
        block_copy(back_send, back_recv, back_sems, to, r).wait_send()
        return carry

    lax.fori_loop(1, regions, finish_sends, 0)
    for step in range(groups):
        for copy in halo_copies(step):
            copy.wait_send()
    for copy in plane_copies:
        copy.wait_send()


def solution(mesh):
    regions = mesh.shape["region"]
    bands = mesh.shape["grp"]

    def shards(ensemble, obs_value, obs_prec, obs_index, obs_count):
        members, rows, columns = ensemble.shape
        slots = obs_index.shape[2]
        cells = rows * TILE
        return pl.pallas_call(
            functools.partial(kernel, regions, bands),
            out_shape=jax.ShapeDtypeStruct(ensemble.shape, BF16),
            in_specs=[pl.BlockSpec(memory_space=pl.ANY)] * 5,
            out_specs=pl.BlockSpec(memory_space=pltpu.VMEM),
            scratch_shapes=[
                pltpu.VMEM((members, rows, columns + 2 * LANES), BF16),
                pltpu.VMEM((members, rows, columns + 2 * LANES), BF16),
                pltpu.VMEM((2, rows, 2 * LANES), BF16),
                pltpu.VMEM((2, rows, 2 * LANES), BF16),
                pltpu.VMEM((regions, 1, slots), jnp.int32),
                pltpu.VMEM((1, 1), jnp.int32),
                pltpu.VMEM((4, members * 8, LANES), F32),
                pltpu.VMEM((regions, members, cells), BF16),
                pltpu.VMEM((regions, members, cells), BF16),
                pltpu.VMEM((regions, members, slots), F32),
                pltpu.VMEM((regions, members, slots), BF16),
                pltpu.VMEM((regions, members, slots), BF16),
                pltpu.VMEM((regions, members, cells), BF16),
                pltpu.VMEM((regions, members, cells), BF16),
                pltpu.SemaphoreType.DMA((5,)),
                pltpu.SemaphoreType.DMA((2, regions // 2)),
                pltpu.SemaphoreType.DMA((2, 4)),
                pltpu.SemaphoreType.DMA((2, regions)),
                pltpu.SemaphoreType.DMA((2, regions)),
                pltpu.SemaphoreType.DMA((2, regions)),
                pltpu.SemaphoreType.DMA((2, regions)),
            ],
            compiler_params=pltpu.CompilerParams(
                collective_id=0, has_side_effects=True, vmem_limit_bytes=60 * 1024 * 1024
            ),
        )(ensemble, obs_value, obs_prec, obs_index, obs_count)

    placed = (
        P("region", "grp", None),
        P("grp", None),
        P("grp", None),
        P("grp", "region", None),
        P("grp", "region"),
    )
    return jax.shard_map(
        shards, mesh=mesh, in_specs=placed, out_specs=P("region", "grp", None), check_vma=False
    )
```

```python
import functools
import math

import jax
import jax.numpy as jnp
from jax import lax
from jax.experimental import pallas as pl
from jax.experimental.pallas import tpu as pltpu
from jax.sharding import PartitionSpec as P

TILE = 32
ITERS = 5
LANES = 128
MESH = pl.DeviceIdType.MESH
F32 = jnp.float32
BF16 = jnp.bfloat16


def swap_blocks(parts):
    lane = lax.broadcasted_iota(jnp.int32, parts[0].shape, 1)
    low = lane < 64
    even = (lane // 32) % 2 == 0
    half = []
    for a, b in ((parts[0], parts[2]), (parts[1], parts[3])):
        half.append(
            (
                jnp.where(low, a, pltpu.roll(b, 64, 1)),
                jnp.where(low, pltpu.roll(a, 64, 1), b),
            )
        )
    result = []
    for which in range(2):
        a, b = half[0][which], half[1][which]
        result.append(jnp.where(even, a, pltpu.roll(b, 32, 1)))
        result.append(jnp.where(even, pltpu.roll(a, 96, 1), b))
    return result


def split(a):
    high = a.astype(BF16)
    return high, (a - high.astype(F32)).astype(BF16)


def product(a, b):
    return (
        jnp.dot(a[0], b[0], preferred_element_type=F32)
        + jnp.dot(a[0], b[1], preferred_element_type=F32)
        + jnp.dot(a[1], b[0], preferred_element_type=F32)
    )


def window_base(tile):
    return jnp.clip((tile * TILE + LANES - TILE // 2) // LANES - 1, 0, 2)


def padded_base(tile):
    return (tile * TILE + LANES - TILE // 2) // LANES


def column_select(cells, tile, first):
    column = cells % (2 * TILE) + (tile * TILE - TILE // 2 - first)
    place = lax.broadcasted_iota(jnp.int32, (2 * LANES, cells.shape[1]), 0)
    return jnp.where(place == column, F32(1.0), F32(0.0)).astype(BF16)


def fold_rows(parts):
    place = lax.broadcasted_iota(jnp.int32, parts[0].shape, 0)
    distance = 1
    while len(parts) > 1:
        odd = (place // distance) % 2 == 1
        parts = [
            jnp.where(odd, b, a) + pltpu.roll(jnp.where(odd, a, b), distance, 0)
            for a, b in zip(parts[::2], parts[1::2])
        ]
        distance *= 2
    return parts[0]


def row_select(columns, rows, members):
    slots = columns.shape[1]
    place = lax.broadcasted_iota(jnp.int32, (8, slots), 0)
    masks = [place + 8 * q == rows for q in range(4)]
    chosen = []
    for m in range(members):
        part = jnp.zeros((8, slots), F32)
        for q in range(4):
            at = m * TILE + 8 * q
            part = jnp.where(masks[q], columns[at : at + 8], part)
        chosen.append(part)
    return jnp.concatenate([fold_rows(chosen[m : m + 8]) for m in range(0, members, 8)], axis=0)


def own_rows(cells):
    return cells // (2 * TILE) - TILE // 2


def halo_rows(cells, first, last):
    row = cells // (2 * TILE)
    above = jnp.where(first, -1, row)
    below = jnp.where(last, -1, row - TILE)
    return jnp.where(row < TILE // 2, above, jnp.where(row >= 3 * TILE // 2, below, -1))


def kernel(
    regions,
    bands,
    ens,
    value,
    precision,
    index,
    count,
    out,
    held,
    halo,
    planes,
    planes_halo,
    cells_all,
    live_count,
    shuffle,
    main_send,
    main_recv,
    selected,
    obs_send,
    obs_recv,
    back_send,
    back_recv,
    load_sems,
    halo_sems,
    plane_sems,
    cell_sems,
    main_sems,
    obs_sems,
    back_sems,
):
    r = lax.axis_index("region")
    g = lax.axis_index("grp")
    up = lax.rem(g + bands - 1, bands)
    down = lax.rem(g + 1, bands)
    members = ens.shape[0]
    total = members * regions
    half = TILE // 2
    slots = index.shape[2]
    columns_all = ens.shape[2]
    groups = regions // 4
    chips = regions // 2
    first_group = r // 4
    chip, core = r // 2, lax.rem(r, 2)

    def peer(d):
        return lax.rem(r + d, regions)

    def ring_order(distances):
        return [
            2 * lax.rem(chip + d % chips, chips) + (1 - core if other else core)
            for d in distances
            for other in (0, 1)
            if d % chips or other
        ]

    barrier = pltpu.get_barrier_semaphore()
    for to in ring_order((4, 3, -3, 2, -2, 1, -1, 0)):
        pl.semaphore_signal(barrier, inc=1, device_id={"region": to}, device_id_type=MESH)
    has_side = (g < bands - 1, g > 0)
    band_peers = (down, up)
    for side in range(2):

        @pl.when(has_side[side])
        def _():
            pl.semaphore_signal(
                barrier, inc=1, device_id={"grp": band_peers[side]}, device_id_type=MESH
            )

    base_lanes = pl.ds(pl.multiple_of(window_base(r) * LANES, LANES), 2 * LANES)
    loads = [
        pltpu.make_async_copy(src, dst, load_sems.at[n])
        for n, (src, dst) in enumerate(
            (
                (ens, held.at[:, :, LANES : LANES + columns_all]),
                (value.at[:, base_lanes], planes.at[0]),
                (precision.at[:, base_lanes], planes.at[1]),
                (index.at[0], cells_all.at[r]),
                (count, live_count),
            )
        )
    ]
    for copy in loads:
        copy.start()
    zeros = jnp.zeros((members, TILE, LANES), BF16)
    for side in (slice(0, LANES), slice(LANES + columns_all, 2 * LANES + columns_all)):
        held[:, :, side] = zeros
        halo[:, :, side] = zeros
    for side in range(2):

        @pl.when(jnp.logical_not(has_side[1 - side]))
        def _():
            halo[:, side * half : (side + 1) * half, :] = jnp.zeros(
                (members, half, columns_all + 2 * LANES), BF16
            )
            planes_halo[:, side * half : (side + 1) * half, :] = jnp.zeros(
                (2, half, 2 * LANES), BF16
            )

    loads[0].wait()

    def group_lanes(group):
        return pl.ds(pl.multiple_of(group * LANES, LANES), LANES)

    def padded_lanes(group):
        return group_lanes(group + 1)

    def pack_group(group, carry):
        lanes = padded_lanes(group)
        for m in range(members):
            block = held[m, :, lanes].astype(F32)
            parts = swap_blocks([block[8 * q : 8 * q + 8] for q in range(4)])
            for t in range(4):
                shuffle[t, m * 8 : m * 8 + 8, :] = parts[t]
        for t in range(4):
            for s in range(8):
                main_send[4 * group + t, :, s * LANES : (s + 1) * LANES] = shuffle[
                    t, pl.ds(s, members, stride=8), :
                ].astype(BF16)
        return carry

    lax.fori_loop(0, groups, pack_group, 0)
    for copy in loads[1:]:
        copy.wait()
    main_recv[r] = main_send[r]
    bands_beside = jnp.where(g > 0, 1, 0) + jnp.where(g < bands - 1, 1, 0)
    pl.semaphore_wait(barrier, regions - 1 + bands_beside)

    def band_copy(src, dst, sems, at, side):
        return pltpu.make_async_remote_copy(
            src_ref=src,
            dst_ref=dst,
            send_sem=sems.at[0, at],
            recv_sem=sems.at[1, at],
            device_id={"grp": band_peers[side]},
            device_id_type=MESH,
        )

    rows_out = (pl.ds(half, half), pl.ds(0, half))
    rows_in = (pl.ds(0, half), pl.ds(half, half))

    def halo_copy(step, side):
        group = lax.rem(first_group + step, groups)
        lanes = padded_lanes(group)
        return band_copy(
            held.at[:, rows_out[side], lanes],
            halo.at[:, rows_in[side], lanes],
            halo_sems,
            2 * group + side,
            side,
        )

    def plane_copy(n, side):
        return band_copy(
            planes.at[n, rows_out[side], :],
            planes_halo.at[n, rows_in[side], :],
            plane_sems,
            2 * n + side,
            side,
        )

    def start_halo():
        for side in range(2):

            @pl.when(has_side[side])
            def _():
                for step in range(groups):
                    halo_copy(step, side).start()
                for n in range(2):
                    plane_copy(n, side).start()

    def receive_halo(step):
        for side in range(2):

            @pl.when(has_side[1 - side])
            def _():
                halo_copy(step, side).wait_recv()

    def receive_planes():
        for side in range(2):

            @pl.when(has_side[1 - side])
            def _():
                for n in range(2):
                    plane_copy(n, side).wait_recv()

    def finish_halo():
        for side in range(2):

            @pl.when(has_side[side])
            def _():
                for step in range(groups):
                    halo_copy(step, side).wait_send()
                for n in range(2):
                    plane_copy(n, side).wait_send()

    def cell_copy(to, slot):
        return pltpu.make_async_remote_copy(
            src_ref=cells_all.at[r],
            dst_ref=cells_all.at[slot],
            send_sem=cell_sems.at[0, to],
            recv_sem=cell_sems.at[1, slot],
            device_id={"region": to},
            device_id_type=MESH,
        )

    def block_copy(send, recv, sems, to, slot):
        return pltpu.make_async_remote_copy(
            src_ref=send.at[to],
            dst_ref=recv.at[slot],
            send_sem=sems.at[0, to],
            recv_sem=sems.at[1, slot],
            device_id={"region": to},
            device_id_type=MESH,
        )

    def send_main(distances):
        for to in ring_order(distances):
            block_copy(main_send, main_recv, main_sems, to, r).start()

    for to in ring_order((4, 3, -3, 2, -2, 1, -1, 0)):
        cell_copy(to, r).start()
    start_halo()
    send_main((4, 3, -3, 1, -1))

    def choose(source, rows, tile):
        base = padded_base(tile)
        lanes = pl.ds(pl.multiple_of(base * LANES, LANES), 2 * LANES)
        columns = jnp.dot(
            source[:, :, lanes].reshape(members * TILE, 2 * LANES),
            column_select(cells_all[tile], tile, (base - 1) * LANES),
            preferred_element_type=F32,
        )
        return row_select(columns, rows, members)

    def tiles_of(step):
        return [peer_tile(4 * step + n) for n in range(4)]

    def peer_tile(n):
        return lax.rem(4 * first_group + 1 + n, regions)

    def from_own(step, carry):
        tiles = tiles_of(step)
        for tile in tiles:

            @pl.when(tile != r)
            def _():
                cell_copy(tile, tile).wait_recv()

        for tile in tiles:
            selected[tile] = choose(held, own_rows(cells_all[tile]), tile)
        return carry

    lax.fori_loop(0, groups, from_own, 0)

    def from_halo(step, carry):
        @pl.when(step == 0)
        def _():
            receive_halo(0)

        @pl.when(step < groups - 1)
        def _():
            receive_halo(step + 1)

        tiles = tiles_of(step)
        for tile in tiles:
            rows = halo_rows(cells_all[tile], g == 0, g == bands - 1)
            obs_send[tile] = (selected[tile] + choose(halo, rows, tile)).astype(BF16)
        for tile in tiles:

            @pl.when(tile != r)
            def _():
                block_copy(obs_send, obs_recv, obs_sems, tile, r).start()

        return carry

    lax.fori_loop(0, groups, from_halo, 0)
    send_main((2, -2, 0))
    obs_recv[r] = obs_send[r]

    receive_planes()
    cells = cells_all[r]
    fields = jnp.concatenate([planes[0], planes_halo[0], planes[1], planes_halo[1]], axis=0)
    columns = jnp.dot(fields, column_select(cells, r, window_base(r) * LANES), preferred_element_type=F32)
    place = lax.broadcasted_iota(jnp.int32, (TILE, slots), 0)
    at_own = place == own_rows(cells)
    at_halo = place == halo_rows(cells, g == 0, g == bands - 1)

    def field(n):
        own = jnp.where(at_own, columns[2 * n * TILE : (2 * n + 1) * TILE], F32(0.0))
        beside = jnp.where(at_halo, columns[(2 * n + 1) * TILE : (2 * n + 2) * TILE], F32(0.0))
        return jnp.sum(own + beside, axis=0, keepdims=True)

    values_at = field(0)
    precision_at = field(1)
    offset_y = (cells // (2 * TILE)).astype(F32) - (TILE - 0.5)
    offset_x = (cells % (2 * TILE)).astype(F32) - (TILE - 0.5)
    length = 0.375 * TILE
    inflation = jnp.exp(-(offset_y * offset_y + offset_x * offset_x) / (2.0 * length * length))
    live = lax.broadcasted_iota(jnp.int32, (1, slots), 1) < live_count[...]
    weight = jnp.where(live, precision_at * inflation, F32(0.0))

    def wait_block(recv, sems):
        def body(d, carry):
            src = peer(d)
            block_copy(recv, recv, sems, src, src).wait_recv()
            return carry

        lax.fori_loop(1, regions, body, 0)

    wait_block(obs_recv, obs_sems)

    raw = obs_recv[...].reshape(total, slots).astype(F32)
    average = jnp.sum(raw, axis=0, keepdims=True) * (1.0 / total)
    pert = (raw - average).astype(BF16)
    scaled = weight * (values_at - average)
    weighted = (pert.astype(F32) * weight).astype(BF16)
    across = (((1,), (1,)), ((), ()))
    diagonal = lax.broadcasted_iota(jnp.int32, (total, total), 0) == lax.broadcasted_iota(
        jnp.int32, (total, total), 1
    )

    def plus_identity(scale, a):
        return a + jnp.where(diagonal, F32(scale), F32(0.0))

    system = plus_identity(
        total - 1.0, lax.dot_general(pert, weighted, across, preferred_element_type=F32)
    )
    squares = jnp.sum(system * system, axis=0, keepdims=True)
    frobenius = jnp.sqrt(jnp.sum(squares, axis=1, keepdims=True))
    inverse_frobenius = 1.0 / frobenius

    scaled_high = scaled.astype(BF16)
    rest = scaled - scaled_high.astype(F32)
    scaled_mid = rest.astype(BF16)
    scaled_low = (rest - scaled_mid.astype(F32)).astype(BF16)

    def stack(*rows):
        n = rows[0].shape[1]
        place = lax.broadcasted_iota(jnp.int32, (16, n), 0)
        whole = jnp.zeros((16, n), F32)
        for at, row in enumerate(rows):
            whole = jnp.where(place == at, row.astype(F32), whole)
        return whole.astype(BF16)

    projected = jnp.sum(
        lax.dot_general(
            stack(scaled_high, scaled_mid, scaled_low), pert, across, preferred_element_type=F32
        ),
        axis=0,
        keepdims=True,
    )

    start = system * inverse_frobenius
    root = split(start)
    inverse_root = plus_identity(1.5, -0.5 * start)
    factor = split(inverse_root)
    inverse_pair = factor
    root = split(product(root, factor))
    for number in range(1, ITERS):
        factor = split(plus_identity(1.5, -0.5 * product(root, inverse_pair)))
        if number < ITERS - 1:
            root = split(product(factor, root))
        inverse_root = product(inverse_pair, factor)
        inverse_pair = split(inverse_root)

    def row_product(row):
        pair = stack(*split(row))
        first = jnp.dot(pair, inverse_pair[0], preferred_element_type=F32)
        second = jnp.dot(pair, inverse_pair[1], preferred_element_type=F32)
        return first[0:1] + first[1:2] + second[0:1]

    mean_weight = row_product(row_product(projected)) * inverse_frobenius
    spread = math.sqrt(total - 1.0) / jnp.sqrt(frobenius)
    weights = (spread * inverse_root + mean_weight).astype(BF16)

    wait_block(main_recv, main_sems)
    cell_total = main_recv.shape[2]
    step = 2 * LANES
    for n in range(cell_total // step):
        at = slice(n * step, (n + 1) * step)
        prior = main_recv[:, :, at].reshape(total, step).astype(F32)
        mean = jnp.sum(prior, axis=0, keepdims=True) * (1.0 / total)
        update = jnp.dot(weights, (prior - mean).astype(BF16), preferred_element_type=F32)
        back_send[:, :, at] = (update + mean).astype(BF16).reshape(regions, members, step)

    for to in ring_order((4, 3, -3, 2, -2, 1, -1, 0)):
        block_copy(back_send, back_recv, back_sems, to, r).start()
    back_recv[r] = back_send[r]

    def unpack_group(step, carry):
        group = lax.rem(first_group + 2 + step, groups)
        lanes = group_lanes(group)
        for t in range(4):
            tile = 4 * group + t

            @pl.when(tile != r)
            def _():
                block_copy(back_recv, back_recv, back_sems, tile, tile).wait_recv()

        for t in range(4):
            for s in range(8):
                shuffle[t, pl.ds(s, members, stride=8), :] = back_recv[
                    4 * group + t, :, s * LANES : (s + 1) * LANES
                ].astype(F32)
        for m in range(members):
            parts = swap_blocks([shuffle[t, m * 8 : m * 8 + 8, :] for t in range(4)])
            out[m, :, lanes] = jnp.concatenate(parts, axis=0).astype(BF16)
        return carry

    lax.fori_loop(0, groups, unpack_group, 0)

    def finish_sends(d, carry):
        to = peer(d)
        cell_copy(to, r).wait_send()
        block_copy(main_send, main_recv, main_sems, to, r).wait_send()
        block_copy(obs_send, obs_recv, obs_sems, to, r).wait_send()
        block_copy(back_send, back_recv, back_sems, to, r).wait_send()
        return carry

    lax.fori_loop(1, regions, finish_sends, 0)
    finish_halo()


def solution(mesh):
    regions = mesh.shape["region"]
    bands = mesh.shape["grp"]

    def shards(ensemble, obs_value, obs_prec, obs_index, obs_count):
        members, rows, columns = ensemble.shape
        slots = obs_index.shape[2]
        cells = rows * TILE
        return pl.pallas_call(
            functools.partial(kernel, regions, bands),
            out_shape=pltpu.VMEM(ensemble.shape, BF16),
            in_specs=[pl.BlockSpec(memory_space=pl.ANY)] * 5,
            out_specs=pl.BlockSpec(memory_space=pltpu.VMEM),
            scratch_shapes=[
                pltpu.VMEM((members, rows, columns + 2 * LANES), BF16),
                pltpu.VMEM((members, rows, columns + 2 * LANES), BF16),
                pltpu.VMEM((2, rows, 2 * LANES), BF16),
                pltpu.VMEM((2, rows, 2 * LANES), BF16),
                pltpu.VMEM((regions, 1, slots), jnp.int32),
                pltpu.VMEM((1, 1), jnp.int32),
                pltpu.VMEM((4, members * 8, LANES), F32),
                pltpu.VMEM((regions, members, cells), BF16),
                pltpu.VMEM((regions, members, cells), BF16),
                pltpu.VMEM((regions, members, slots), F32),
                pltpu.VMEM((regions, members, slots), BF16),
                pltpu.VMEM((regions, members, slots), BF16),
                pltpu.VMEM((regions, members, cells), BF16),
                pltpu.VMEM((regions, members, cells), BF16),
                pltpu.SemaphoreType.DMA((5,)),
                pltpu.SemaphoreType.DMA((2, regions // 2)),
                pltpu.SemaphoreType.DMA((2, 4)),
                pltpu.SemaphoreType.DMA((2, regions)),
                pltpu.SemaphoreType.DMA((2, regions)),
                pltpu.SemaphoreType.DMA((2, regions)),
                pltpu.SemaphoreType.DMA((2, regions)),
            ],
            compiler_params=pltpu.CompilerParams(
                collective_id=0, has_side_effects=True, vmem_limit_bytes=60 * 1024 * 1024
            ),
        )(ensemble, obs_value, obs_prec, obs_index, obs_count)

    placed = (
        P("region", "grp", None),
        P("grp", None),
        P("grp", None),
        P("grp", "region", None),
        P("grp", "region"),
    )
    return jax.shard_map(
        shards, mesh=mesh, in_specs=placed, out_specs=P("region", "grp", None), check_vma=False
    )
```

```python
import functools
import math

import jax
import jax.numpy as jnp
from jax import lax
from jax.experimental import pallas as pl
from jax.experimental.pallas import tpu as pltpu
from jax.sharding import PartitionSpec as P

TILE = 32
ITERS = 5
LANES = 128
START = 1
MESH = pl.DeviceIdType.MESH
F32 = jnp.float32
BF16 = jnp.bfloat16


def swap_blocks(parts):
    lane = lax.broadcasted_iota(jnp.int32, parts[0].shape, 1)
    low = lane < 64
    even = (lane // 32) % 2 == 0
    half = []
    for a, b in ((parts[0], parts[2]), (parts[1], parts[3])):
        half.append(
            (
                jnp.where(low, a, pltpu.roll(b, 64, 1)),
                jnp.where(low, pltpu.roll(a, 64, 1), b),
            )
        )
    result = []
    for which in range(2):
        a, b = half[0][which], half[1][which]
        result.append(jnp.where(even, a, pltpu.roll(b, 32, 1)))
        result.append(jnp.where(even, pltpu.roll(a, 96, 1), b))
    return result


def split(a):
    high = a.astype(BF16)
    return high, (a - high.astype(F32)).astype(BF16)


def product(a, b):
    return (
        jnp.dot(a[0], b[0], preferred_element_type=F32)
        + jnp.dot(a[0], b[1], preferred_element_type=F32)
        + jnp.dot(a[1], b[0], preferred_element_type=F32)
    )


def window_base(tile):
    return jnp.clip((tile * TILE + LANES - TILE // 2) // LANES - 1, 0, 2)


def padded_base(tile):
    return (tile * TILE + LANES - TILE // 2) // LANES


def column_select(cells, tile, first, width):
    column = cells % (2 * TILE) + (tile * TILE - TILE // 2 - first)
    place = lax.broadcasted_iota(jnp.int32, (width, cells.shape[1]), 0)
    return jnp.where(place == column, F32(1.0), F32(0.0)).astype(BF16)


def fold_rows(parts):
    place = lax.broadcasted_iota(jnp.int32, parts[0].shape, 0)
    distance = 1
    while len(parts) > 1:
        odd = (place // distance) % 2 == 1
        parts = [
            jnp.where(odd, b, a) + pltpu.roll(jnp.where(odd, a, b), distance, 0)
            for a, b in zip(parts[::2], parts[1::2])
        ]
        distance *= 2
    return parts[0]


def row_select(columns, rows, members):
    slots = columns.shape[1]
    place = lax.broadcasted_iota(jnp.int32, (8, slots), 0)
    masks = [place + 8 * q == rows for q in range(4)]
    chosen = []
    for m in range(members):
        part = jnp.zeros((8, slots), F32)
        for q in range(4):
            at = m * TILE + 8 * q
            part = jnp.where(masks[q], columns[at : at + 8], part)
        chosen.append(part)
    return jnp.concatenate([fold_rows(chosen[m : m + 8]) for m in range(0, members, 8)], axis=0)


def own_rows(cells):
    return cells // (2 * TILE) - TILE // 2


def halo_rows(cells, first, last):
    row = cells // (2 * TILE)
    above = jnp.where(first, -1, row)
    below = jnp.where(last, -1, row - TILE)
    return jnp.where(row < TILE // 2, above, jnp.where(row >= 3 * TILE // 2, below, -1))


def kernel(
    regions,
    bands,
    ens,
    value,
    precision,
    index,
    count,
    out,
    held,
    halo,
    planes,
    planes_halo,
    cells_all,
    live_count,
    shuffle,
    main_send,
    main_recv,
    selected,
    obs_send,
    obs_recv,
    back_send,
    back_recv,
    load_sems,
    halo_sems,
    plane_sems,
    cell_sems,
    main_sems,
    obs_sems,
    back_sems,
):
    r = lax.axis_index("region")
    g = lax.axis_index("grp")
    up = lax.rem(g + bands - 1, bands)
    down = lax.rem(g + 1, bands)
    members = ens.shape[0]
    total = members * regions
    half = TILE // 2
    slots = index.shape[2]
    columns_all = ens.shape[2]
    groups = regions // 4
    chips = regions // 2
    first_group = r // 4
    chip, core = r // 2, lax.rem(r, 2)

    def peer(d):
        return lax.rem(r + d, regions)

    def ring_order(distances):
        return [
            2 * lax.rem(chip + d % chips, chips) + (1 - core if other else core)
            for d in distances
            for other in (0, 1)
            if d % chips or other
        ]

    barrier = pltpu.get_barrier_semaphore()
    for to in ring_order((4, 3, -3, 2, -2, 1, -1, 0)):
        pl.semaphore_signal(barrier, inc=1, device_id={"region": to}, device_id_type=MESH)
    has_side = (g < bands - 1, g > 0)
    band_peers = (down, up)
    for side in range(2):

        @pl.when(has_side[side])
        def _():
            pl.semaphore_signal(
                barrier, inc=1, device_id={"grp": band_peers[side]}, device_id_type=MESH
            )

    base_lanes = pl.ds(pl.multiple_of(window_base(r) * LANES, LANES), 2 * LANES)
    loads = [
        pltpu.make_async_copy(src, dst, load_sems.at[n])
        for n, (src, dst) in enumerate(
            (
                (ens, held.at[:, :, LANES : LANES + columns_all]),
                (value.at[:, base_lanes], planes.at[0]),
                (precision.at[:, base_lanes], planes.at[1]),
                (index.at[0], cells_all.at[r]),
                (count, live_count),
            )
        )
    ]
    for copy in loads:
        copy.start()
    zeros = jnp.zeros((members, TILE, LANES), BF16)
    for side in (slice(0, LANES), slice(LANES + columns_all, 2 * LANES + columns_all)):
        held[:, :, side] = zeros
        halo[:, :, side] = zeros
    for side in range(2):

        @pl.when(jnp.logical_not(has_side[1 - side]))
        def _():
            halo[:, side * half : (side + 1) * half, :] = jnp.zeros(
                (members, half, columns_all + 2 * LANES), BF16
            )
            planes_halo[:, side * half : (side + 1) * half, :] = jnp.zeros(
                (2, half, 2 * LANES), BF16
            )

    loads[0].wait()

    def group_lanes(group):
        return pl.ds(pl.multiple_of(group * LANES, LANES), LANES)

    def padded_lanes(group):
        return group_lanes(group + 1)

    def pack_group(group, carry):
        lanes = padded_lanes(group)
        for m in range(members):
            block = held[m, :, lanes].astype(F32)
            parts = swap_blocks([block[8 * q : 8 * q + 8] for q in range(4)])
            for t in range(4):
                shuffle[t, m * 8 : m * 8 + 8, :] = parts[t]
        for t in range(4):
            for s in range(8):
                main_send[4 * group + t, :, s * LANES : (s + 1) * LANES] = shuffle[
                    t, pl.ds(s, members, stride=8), :
                ].astype(BF16)
        return carry

    lax.fori_loop(0, groups, pack_group, 0)
    for copy in loads[1:]:
        copy.wait()
    main_recv[r] = main_send[r]
    bands_beside = jnp.where(g > 0, 1, 0) + jnp.where(g < bands - 1, 1, 0)
    pl.semaphore_wait(barrier, regions - 1 + bands_beside)

    def band_copy(src, dst, sems, at, side):
        return pltpu.make_async_remote_copy(
            src_ref=src,
            dst_ref=dst,
            send_sem=sems.at[0, at],
            recv_sem=sems.at[1, at],
            device_id={"grp": band_peers[side]},
            device_id_type=MESH,
        )

    rows_out = (pl.ds(half, half), pl.ds(0, half))
    rows_in = (pl.ds(0, half), pl.ds(half, half))

    def halo_copy(step, side):
        group = lax.rem(first_group + START + step, groups)
        lanes = padded_lanes(group)
        return band_copy(
            held.at[:, rows_out[side], lanes],
            halo.at[:, rows_in[side], lanes],
            halo_sems,
            2 * group + side,
            side,
        )

    def plane_copy(n, side):
        return band_copy(
            planes.at[n, rows_out[side], :],
            planes_halo.at[n, rows_in[side], :],
            plane_sems,
            2 * n + side,
            side,
        )

    def start_halo():
        for side in range(2):

            @pl.when(has_side[side])
            def _():
                for step in range(groups):
                    halo_copy(step, side).start()
                for n in range(2):
                    plane_copy(n, side).start()

    def receive_halo(step):
        for side in range(2):

            @pl.when(has_side[1 - side])
            def _():
                halo_copy(step, side).wait_recv()

    def receive_planes():
        for side in range(2):

            @pl.when(has_side[1 - side])
            def _():
                for n in range(2):
                    plane_copy(n, side).wait_recv()

    def finish_halo():
        for side in range(2):

            @pl.when(has_side[side])
            def _():
                for step in range(groups):
                    halo_copy(step, side).wait_send()
                for n in range(2):
                    plane_copy(n, side).wait_send()

    def cell_copy(to, slot):
        return pltpu.make_async_remote_copy(
            src_ref=cells_all.at[r],
            dst_ref=cells_all.at[slot],
            send_sem=cell_sems.at[0, to],
            recv_sem=cell_sems.at[1, slot],
            device_id={"region": to},
            device_id_type=MESH,
        )

    def block_copy(send, recv, sems, to, slot):
        return pltpu.make_async_remote_copy(
            src_ref=send.at[to],
            dst_ref=recv.at[slot],
            send_sem=sems.at[0, to],
            recv_sem=sems.at[1, slot],
            device_id={"region": to},
            device_id_type=MESH,
        )

    def send_main(distances):
        for to in ring_order(distances):
            block_copy(main_send, main_recv, main_sems, to, r).start()

    start_halo()
    for to in ring_order((4, 3, -3, 2, -2, 1, -1, 0)):
        cell_copy(to, r).start()
    send_main((3, -3, 2, -2))

    def choose(source, rows, tile, kind):
        one_block = kind in (1, 2)
        base = tile // 4 + 1 if one_block else padded_base(tile)
        width = LANES if one_block else 2 * LANES
        lanes = pl.ds(pl.multiple_of(base * LANES, LANES), width)
        columns = jnp.dot(
            source[:, :, lanes].reshape(members * TILE, width),
            column_select(cells_all[tile], tile, (base - 1) * LANES, width),
            preferred_element_type=F32,
        )
        return row_select(columns, rows, members)

    def from_own(step, carry):
        group = lax.rem(first_group + jnp.where(step < 2, step, 5 - step), groups)
        for kind in range(4):
            tile = 4 * group + kind

            @pl.when(tile != r)
            def _():
                cell_copy(tile, tile).wait_recv()

        for kind in range(4):
            tile = 4 * group + kind
            selected[tile] = choose(held, own_rows(cells_all[tile]), tile, kind)
        return carry

    lax.fori_loop(0, groups, from_own, 0)

    for step, places in enumerate((range(2), range(2, 6), range(6, 10), range(10, 16))):
        receive_halo(step)
        tiles = [(lax.rem(4 * (first_group + START) + 1 + n, regions), (1 + n) % 4) for n in places]
        for tile, kind in tiles:
            rows = halo_rows(cells_all[tile], g == 0, g == bands - 1)
            obs_send[tile] = (selected[tile] + choose(halo, rows, tile, kind)).astype(BF16)
        for tile, _ in tiles:

            @pl.when(tile != r)
            def _():
                block_copy(obs_send, obs_recv, obs_sems, tile, r).start()

    send_main((4, 1, -1, 0))
    obs_recv[r] = obs_send[r]

    receive_planes()
    cells = cells_all[r]
    fields = jnp.concatenate([planes[0], planes_halo[0], planes[1], planes_halo[1]], axis=0)
    columns = jnp.dot(fields, column_select(cells, r, window_base(r) * LANES, 2 * LANES), preferred_element_type=F32)
    place = lax.broadcasted_iota(jnp.int32, (TILE, slots), 0)
    at_own = place == own_rows(cells)
    at_halo = place == halo_rows(cells, g == 0, g == bands - 1)

    def field(n):
        own = jnp.where(at_own, columns[2 * n * TILE : (2 * n + 1) * TILE], F32(0.0))
        beside = jnp.where(at_halo, columns[(2 * n + 1) * TILE : (2 * n + 2) * TILE], F32(0.0))
        return jnp.sum(own + beside, axis=0, keepdims=True)

    values_at = field(0)
    precision_at = field(1)
    offset_y = (cells // (2 * TILE)).astype(F32) - (TILE - 0.5)
    offset_x = (cells % (2 * TILE)).astype(F32) - (TILE - 0.5)
    length = 0.375 * TILE
    inflation = jnp.exp(-(offset_y * offset_y + offset_x * offset_x) / (2.0 * length * length))
    live = lax.broadcasted_iota(jnp.int32, (1, slots), 1) < live_count[...]
    weight = jnp.where(live, precision_at * inflation, F32(0.0))

    def wait_block(recv, sems):
        def body(d, carry):
            src = peer(d)
            block_copy(recv, recv, sems, src, src).wait_recv()
            return carry

        lax.fori_loop(1, regions, body, 0)

    wait_block(obs_recv, obs_sems)

    raw = obs_recv[...].reshape(total, slots).astype(F32)
    average = jnp.sum(raw, axis=0, keepdims=True) * (1.0 / total)
    pert = (raw - average).astype(BF16)
    scaled = weight * (values_at - average)
    weighted = (pert.astype(F32) * weight).astype(BF16)
    across = (((1,), (1,)), ((), ()))
    diagonal = lax.broadcasted_iota(jnp.int32, (total, total), 0) == lax.broadcasted_iota(
        jnp.int32, (total, total), 1
    )

    def plus_identity(scale, a):
        return a + jnp.where(diagonal, F32(scale), F32(0.0))

    system = plus_identity(
        total - 1.0, lax.dot_general(pert, weighted, across, preferred_element_type=F32)
    )
    squares = jnp.sum(system * system, axis=0, keepdims=True)
    frobenius = jnp.sqrt(jnp.sum(squares, axis=1, keepdims=True))
    inverse_frobenius = 1.0 / frobenius

    scaled_high = scaled.astype(BF16)
    rest = scaled - scaled_high.astype(F32)
    scaled_mid = rest.astype(BF16)
    scaled_low = (rest - scaled_mid.astype(F32)).astype(BF16)

    def stack(*rows):
        n = rows[0].shape[1]
        place = lax.broadcasted_iota(jnp.int32, (16, n), 0)
        whole = jnp.zeros((16, n), F32)
        for at, row in enumerate(rows):
            whole = jnp.where(place == at, row.astype(F32), whole)
        return whole.astype(BF16)

    projected = jnp.sum(
        lax.dot_general(
            stack(scaled_high, scaled_mid, scaled_low), pert, across, preferred_element_type=F32
        ),
        axis=0,
        keepdims=True,
    )

    start = system * inverse_frobenius
    root = split(start)
    inverse_root = plus_identity(1.5, -0.5 * start)
    factor = split(inverse_root)
    inverse_pair = factor
    root = split(product(root, factor))
    for number in range(1, ITERS):
        factor = split(plus_identity(1.5, -0.5 * product(root, inverse_pair)))
        if number < ITERS - 1:
            root = split(product(factor, root))
        inverse_root = product(inverse_pair, factor)
        inverse_pair = split(inverse_root)

    def row_product(row):
        pair = stack(*split(row))
        first = jnp.dot(pair, inverse_pair[0], preferred_element_type=F32)
        second = jnp.dot(pair, inverse_pair[1], preferred_element_type=F32)
        return first[0:1] + first[1:2] + second[0:1]

    mean_weight = row_product(row_product(projected)) * inverse_frobenius
    spread = math.sqrt(total - 1.0) / jnp.sqrt(frobenius)
    weights = (spread * inverse_root + mean_weight).astype(BF16)

    wait_block(main_recv, main_sems)
    cell_total = main_recv.shape[2]
    step = 2 * LANES
    for n in range(cell_total // step):
        at = slice(n * step, (n + 1) * step)
        prior = main_recv[:, :, at].reshape(total, step).astype(F32)
        mean = jnp.sum(prior, axis=0, keepdims=True) * (1.0 / total)
        update = jnp.dot(weights, (prior - mean).astype(BF16), preferred_element_type=F32)
        back_send[:, :, at] = (update + mean).astype(BF16).reshape(regions, members, step)

    for to in ring_order((1, -1, 2, -2, 3, -3, 4, 0)):
        block_copy(back_send, back_recv, back_sems, to, r).start()
    back_recv[r] = back_send[r]

    def unpack_group(step, carry):
        group = lax.rem(first_group + step, groups)
        lanes = group_lanes(group)
        for t in range(4):
            tile = 4 * group + t

            @pl.when(tile != r)
            def _():
                block_copy(back_recv, back_recv, back_sems, tile, tile).wait_recv()

        for t in range(4):
            for s in range(8):
                shuffle[t, pl.ds(s, members, stride=8), :] = back_recv[
                    4 * group + t, :, s * LANES : (s + 1) * LANES
                ].astype(F32)
        for m in range(members):
            parts = swap_blocks([shuffle[t, m * 8 : m * 8 + 8, :] for t in range(4)])
            out[m, :, lanes] = jnp.concatenate(parts, axis=0).astype(BF16)
        return carry

    lax.fori_loop(0, groups, unpack_group, 0)

    def finish_sends(d, carry):
        to = peer(d)
        cell_copy(to, r).wait_send()
        block_copy(main_send, main_recv, main_sems, to, r).wait_send()
        block_copy(obs_send, obs_recv, obs_sems, to, r).wait_send()
        block_copy(back_send, back_recv, back_sems, to, r).wait_send()
        return carry

    lax.fori_loop(1, regions, finish_sends, 0)
    finish_halo()


def solution(mesh):
    regions = mesh.shape["region"]
    bands = mesh.shape["grp"]

    def shards(ensemble, obs_value, obs_prec, obs_index, obs_count):
        members, rows, columns = ensemble.shape
        slots = obs_index.shape[2]
        cells = rows * TILE
        return pl.pallas_call(
            functools.partial(kernel, regions, bands),
            out_shape=pltpu.VMEM(ensemble.shape, BF16),
            in_specs=[pl.BlockSpec(memory_space=pl.ANY)] * 5,
            out_specs=pl.BlockSpec(memory_space=pltpu.VMEM),
            scratch_shapes=[
                pltpu.VMEM((members, rows, columns + 2 * LANES), BF16),
                pltpu.VMEM((members, rows, columns + 2 * LANES), BF16),
                pltpu.VMEM((2, rows, 2 * LANES), BF16),
                pltpu.VMEM((2, rows, 2 * LANES), BF16),
                pltpu.VMEM((regions, 1, slots), jnp.int32),
                pltpu.VMEM((1, 1), jnp.int32),
                pltpu.VMEM((4, members * 8, LANES), F32),
                pltpu.VMEM((regions, members, cells), BF16),
                pltpu.VMEM((regions, members, cells), BF16),
                pltpu.VMEM((regions, members, slots), F32),
                pltpu.VMEM((regions, members, slots), BF16),
                pltpu.VMEM((regions, members, slots), BF16),
                pltpu.VMEM((regions, members, cells), BF16),
                pltpu.VMEM((regions, members, cells), BF16),
                pltpu.SemaphoreType.DMA((5,)),
                pltpu.SemaphoreType.DMA((2, regions // 2)),
                pltpu.SemaphoreType.DMA((2, 4)),
                pltpu.SemaphoreType.DMA((2, regions)),
                pltpu.SemaphoreType.DMA((2, regions)),
                pltpu.SemaphoreType.DMA((2, regions)),
                pltpu.SemaphoreType.DMA((2, regions)),
            ],
            compiler_params=pltpu.CompilerParams(
                collective_id=0, has_side_effects=True, vmem_limit_bytes=60 * 1024 * 1024
            ),
        )(ensemble, obs_value, obs_prec, obs_index, obs_count)

    placed = (
        P("region", "grp", None),
        P("grp", None),
        P("grp", None),
        P("grp", "region", None),
        P("grp", "region"),
    )
    return jax.shard_map(
        shards, mesh=mesh, in_specs=placed, out_specs=P("region", "grp", None), check_vma=False
    )
```

```python
import functools
import math

import jax
import jax.numpy as jnp
from jax import lax
from jax.experimental import pallas as pl
from jax.experimental.pallas import tpu as pltpu
from jax.sharding import PartitionSpec as P

TILE = 32
ITERS = 5
LANES = 128
START = 1
MESH = pl.DeviceIdType.MESH
F32 = jnp.float32
BF16 = jnp.bfloat16


def swap_blocks(parts):
    lane = lax.broadcasted_iota(jnp.int32, parts[0].shape, 1)
    low = lane < 64
    even = (lane // 32) % 2 == 0
    half = []
    for a, b in ((parts[0], parts[2]), (parts[1], parts[3])):
        half.append(
            (
                jnp.where(low, a, pltpu.roll(b, 64, 1)),
                jnp.where(low, pltpu.roll(a, 64, 1), b),
            )
        )
    result = []
    for which in range(2):
        a, b = half[0][which], half[1][which]
        result.append(jnp.where(even, a, pltpu.roll(b, 32, 1)))
        result.append(jnp.where(even, pltpu.roll(a, 96, 1), b))
    return result


def split(a):
    high = a.astype(BF16)
    return high, (a - high.astype(F32)).astype(BF16)


def product(a, b):
    height = a[0].shape[0] // 2
    blocks = []
    for n in range(2):
        rows = slice(n * height, (n + 1) * height)
        blocks.append(
            jnp.dot(a[0][rows], b[0], preferred_element_type=F32)
            + jnp.dot(a[0][rows], b[1], preferred_element_type=F32)
            + jnp.dot(a[1][rows], b[0], preferred_element_type=F32)
        )
    return jnp.concatenate(blocks, axis=0)


def window_base(tile):
    return jnp.clip((tile * TILE + LANES - TILE // 2) // LANES - 1, 0, 2)


def padded_base(tile):
    return (tile * TILE + LANES - TILE // 2) // LANES


def column_select(cells, tile, first, width):
    column = cells % (2 * TILE) + (tile * TILE - TILE // 2 - first)
    place = lax.broadcasted_iota(jnp.int32, (width, cells.shape[1]), 0)
    return jnp.where(place == column, F32(1.0), F32(0.0)).astype(BF16)


def fold_rows(parts):
    place = lax.broadcasted_iota(jnp.int32, parts[0].shape, 0)
    distance = 1
    while len(parts) > 1:
        odd = (place // distance) % 2 == 1
        parts = [
            jnp.where(odd, b, a) + pltpu.roll(jnp.where(odd, a, b), distance, 0)
            for a, b in zip(parts[::2], parts[1::2])
        ]
        distance *= 2
    return parts[0]


def row_select(columns, rows, members):
    slots = columns.shape[1]
    place = lax.broadcasted_iota(jnp.int32, (8, slots), 0)
    masks = [place + 8 * q == rows for q in range(4)]
    chosen = []
    for m in range(members):
        part = jnp.zeros((8, slots), F32)
        for q in range(4):
            at = m * TILE + 8 * q
            part = jnp.where(masks[q], columns[at : at + 8], part)
        chosen.append(part)
    return jnp.concatenate([fold_rows(chosen[m : m + 8]) for m in range(0, members, 8)], axis=0)


def own_rows(cells):
    return cells // (2 * TILE) - TILE // 2


def halo_rows(cells, first, last):
    row = cells // (2 * TILE)
    above = jnp.where(first, -1, row)
    below = jnp.where(last, -1, row - TILE)
    return jnp.where(row < TILE // 2, above, jnp.where(row >= 3 * TILE // 2, below, -1))


def kernel(
    regions,
    bands,
    ens,
    value,
    precision,
    index,
    count,
    out,
    held,
    halo,
    planes,
    planes_halo,
    cells_all,
    live_count,
    shuffle,
    main_send,
    main_recv,
    selected,
    obs_send,
    obs_recv,
    back_send,
    back_recv,
    load_sems,
    halo_sems,
    plane_sems,
    cell_sems,
    main_sems,
    obs_sems,
    back_sems,
):
    r = lax.axis_index("region")
    g = lax.axis_index("grp")
    up = lax.rem(g + bands - 1, bands)
    down = lax.rem(g + 1, bands)
    members = ens.shape[0]
    total = members * regions
    half = TILE // 2
    slots = index.shape[2]
    columns_all = ens.shape[2]
    groups = regions // 4
    chips = regions // 2
    first_group = r // 4
    chip, core = r // 2, lax.rem(r, 2)

    def peer(d):
        return lax.rem(r + d, regions)

    def ring_order(distances):
        return [
            2 * lax.rem(chip + d % chips, chips) + (1 - core if other else core)
            for d in distances
            for other in (0, 1)
            if d % chips or other
        ]

    barrier = pltpu.get_barrier_semaphore()
    for to in ring_order((4, 3, -3, 2, -2, 1, -1, 0)):
        pl.semaphore_signal(barrier, inc=1, device_id={"region": to}, device_id_type=MESH)
    has_side = (g < bands - 1, g > 0)
    band_peers = (down, up)
    for side in range(2):

        @pl.when(has_side[side])
        def _():
            pl.semaphore_signal(
                barrier, inc=1, device_id={"grp": band_peers[side]}, device_id_type=MESH
            )

    base_lanes = pl.ds(pl.multiple_of(window_base(r) * LANES, LANES), 2 * LANES)
    loads = [
        pltpu.make_async_copy(src, dst, load_sems.at[n])
        for n, (src, dst) in enumerate(
            (
                (ens, held.at[:, :, LANES : LANES + columns_all]),
                (value.at[:, base_lanes], planes.at[0]),
                (precision.at[:, base_lanes], planes.at[1]),
                (index.at[0], cells_all.at[r]),
                (count, live_count),
            )
        )
    ]
    for copy in loads:
        copy.start()
    zeros = jnp.zeros((members, TILE, LANES), BF16)
    for side in (slice(0, LANES), slice(LANES + columns_all, 2 * LANES + columns_all)):
        held[:, :, side] = zeros
        halo[:, :, side] = zeros
    for side in range(2):

        @pl.when(jnp.logical_not(has_side[1 - side]))
        def _():
            halo[:, side * half : (side + 1) * half, :] = jnp.zeros(
                (members, half, columns_all + 2 * LANES), BF16
            )
            planes_halo[:, side * half : (side + 1) * half, :] = jnp.zeros(
                (2, half, 2 * LANES), BF16
            )

    loads[0].wait()

    def group_lanes(group):
        return pl.ds(pl.multiple_of(group * LANES, LANES), LANES)

    def padded_lanes(group):
        return group_lanes(group + 1)

    def pack_group(group, carry):
        lanes = padded_lanes(group)
        for m in range(members):
            block = held[m, :, lanes].astype(F32)
            parts = swap_blocks([block[8 * q : 8 * q + 8] for q in range(4)])
            for t in range(4):
                shuffle[t, m * 8 : m * 8 + 8, :] = parts[t]
        for t in range(4):
            for s in range(8):
                main_send[4 * group + t, :, s * LANES : (s + 1) * LANES] = shuffle[
                    t, pl.ds(s, members, stride=8), :
                ].astype(BF16)
        return carry

    lax.fori_loop(0, groups, pack_group, 0)
    for copy in loads[1:]:
        copy.wait()
    main_recv[r] = main_send[r]
    bands_beside = jnp.where(g > 0, 1, 0) + jnp.where(g < bands - 1, 1, 0)
    pl.semaphore_wait(barrier, regions - 1 + bands_beside)

    def band_copy(src, dst, sems, at, side):
        return pltpu.make_async_remote_copy(
            src_ref=src,
            dst_ref=dst,
            send_sem=sems.at[0, at],
            recv_sem=sems.at[1, at],
            device_id={"grp": band_peers[side]},
            device_id_type=MESH,
        )

    rows_out = (pl.ds(half, half), pl.ds(0, half))
    rows_in = (pl.ds(0, half), pl.ds(half, half))

    def halo_copy(step, side):
        group = lax.rem(first_group + START + step, groups)
        lanes = padded_lanes(group)
        return band_copy(
            held.at[:, rows_out[side], lanes],
            halo.at[:, rows_in[side], lanes],
            halo_sems,
            2 * group + side,
            side,
        )

    def plane_copy(n, side):
        return band_copy(
            planes.at[n, rows_out[side], :],
            planes_halo.at[n, rows_in[side], :],
            plane_sems,
            2 * n + side,
            side,
        )

    def start_halo():
        for side in range(2):

            @pl.when(has_side[side])
            def _():
                for step in range(groups):
                    halo_copy(step, side).start()
                for n in range(2):
                    plane_copy(n, side).start()

    def receive_halo(step):
        for side in range(2):

            @pl.when(has_side[1 - side])
            def _():
                halo_copy(step, side).wait_recv()

    def receive_planes():
        for side in range(2):

            @pl.when(has_side[1 - side])
            def _():
                for n in range(2):
                    plane_copy(n, side).wait_recv()

    def finish_halo():
        for side in range(2):

            @pl.when(has_side[side])
            def _():
                for step in range(groups):
                    halo_copy(step, side).wait_send()
                for n in range(2):
                    plane_copy(n, side).wait_send()

    def cell_copy(to, slot):
        return pltpu.make_async_remote_copy(
            src_ref=cells_all.at[r],
            dst_ref=cells_all.at[slot],
            send_sem=cell_sems.at[0, to],
            recv_sem=cell_sems.at[1, slot],
            device_id={"region": to},
            device_id_type=MESH,
        )

    def block_copy(send, recv, sems, to, slot):
        return pltpu.make_async_remote_copy(
            src_ref=send.at[to],
            dst_ref=recv.at[slot],
            send_sem=sems.at[0, to],
            recv_sem=sems.at[1, slot],
            device_id={"region": to},
            device_id_type=MESH,
        )

    def send_main(distances):
        for to in ring_order(distances):
            block_copy(main_send, main_recv, main_sems, to, r).start()

    start_halo()
    for to in ring_order((4, 3, -3, 2, -2, 1, -1, 0)):
        cell_copy(to, r).start()
    send_main((3, -3, 2, -2))

    def choose(source, rows, tile, kind):
        one_block = kind in (1, 2)
        base = tile // 4 + 1 if one_block else padded_base(tile)
        width = LANES if one_block else 2 * LANES
        lanes = pl.ds(pl.multiple_of(base * LANES, LANES), width)
        columns = jnp.dot(
            source[:, :, lanes].reshape(members * TILE, width),
            column_select(cells_all[tile], tile, (base - 1) * LANES, width),
            preferred_element_type=F32,
        )
        return row_select(columns, rows, members)

    def from_own(step, carry):
        group = lax.rem(first_group + jnp.where(step < 2, step, 5 - step), groups)
        for kind in range(4):
            tile = 4 * group + kind

            @pl.when(tile != r)
            def _():
                cell_copy(tile, tile).wait_recv()

        for kind in range(4):
            tile = 4 * group + kind
            selected[tile] = choose(held, own_rows(cells_all[tile]), tile, kind)
        return carry

    lax.fori_loop(0, groups, from_own, 0)

    for step, places in enumerate((range(2), range(2, 6), range(6, 10), range(10, 16))):
        receive_halo(step)
        tiles = [(lax.rem(4 * (first_group + START) + 1 + n, regions), (1 + n) % 4) for n in places]
        for tile, kind in tiles:
            rows = halo_rows(cells_all[tile], g == 0, g == bands - 1)
            obs_send[tile] = (selected[tile] + choose(halo, rows, tile, kind)).astype(BF16)
        for tile, _ in tiles:

            @pl.when(tile != r)
            def _():
                block_copy(obs_send, obs_recv, obs_sems, tile, r).start()

    send_main((4, 1, -1, 0))
    obs_recv[r] = obs_send[r]

    receive_planes()
    cells = cells_all[r]
    fields = jnp.concatenate([planes[0], planes_halo[0], planes[1], planes_halo[1]], axis=0)
    columns = jnp.dot(fields, column_select(cells, r, window_base(r) * LANES, 2 * LANES), preferred_element_type=F32)
    place = lax.broadcasted_iota(jnp.int32, (TILE, slots), 0)
    at_own = place == own_rows(cells)
    at_halo = place == halo_rows(cells, g == 0, g == bands - 1)

    def field(n):
        own = jnp.where(at_own, columns[2 * n * TILE : (2 * n + 1) * TILE], F32(0.0))
        beside = jnp.where(at_halo, columns[(2 * n + 1) * TILE : (2 * n + 2) * TILE], F32(0.0))
        return jnp.sum(own + beside, axis=0, keepdims=True)

    values_at = field(0)
    precision_at = field(1)
    offset_y = (cells // (2 * TILE)).astype(F32) - (TILE - 0.5)
    offset_x = (cells % (2 * TILE)).astype(F32) - (TILE - 0.5)
    length = 0.375 * TILE
    inflation = jnp.exp(-(offset_y * offset_y + offset_x * offset_x) / (2.0 * length * length))
    live = lax.broadcasted_iota(jnp.int32, (1, slots), 1) < live_count[...]
    weight = jnp.where(live, precision_at * inflation, F32(0.0))

    def wait_block(recv, sems):
        def body(d, carry):
            src = peer(d)
            block_copy(recv, recv, sems, src, src).wait_recv()
            return carry

        lax.fori_loop(1, regions, body, 0)

    wait_block(obs_recv, obs_sems)

    raw = obs_recv[...].reshape(total, slots).astype(F32)
    average = jnp.sum(raw, axis=0, keepdims=True) * (1.0 / total)
    pert = (raw - average).astype(BF16)
    scaled = weight * (values_at - average)
    weighted = (pert.astype(F32) * weight).astype(BF16)
    across = (((1,), (1,)), ((), ()))
    diagonal = lax.broadcasted_iota(jnp.int32, (total, total), 0) == lax.broadcasted_iota(
        jnp.int32, (total, total), 1
    )

    def plus_identity(scale, a):
        return a + jnp.where(diagonal, F32(scale), F32(0.0))

    system = plus_identity(
        total - 1.0, lax.dot_general(pert, weighted, across, preferred_element_type=F32)
    )
    squares = jnp.sum(system * system, axis=0, keepdims=True)
    frobenius = jnp.sqrt(jnp.sum(squares, axis=1, keepdims=True))
    inverse_frobenius = 1.0 / frobenius

    scaled_high = scaled.astype(BF16)
    rest = scaled - scaled_high.astype(F32)
    scaled_mid = rest.astype(BF16)
    scaled_low = (rest - scaled_mid.astype(F32)).astype(BF16)

    def stack(*rows):
        n = rows[0].shape[1]
        place = lax.broadcasted_iota(jnp.int32, (16, n), 0)
        whole = jnp.zeros((16, n), F32)
        for at, row in enumerate(rows):
            whole = jnp.where(place == at, row.astype(F32), whole)
        return whole.astype(BF16)

    projected = jnp.sum(
        lax.dot_general(
            stack(scaled_high, scaled_mid, scaled_low), pert, across, preferred_element_type=F32
        ),
        axis=0,
        keepdims=True,
    )

    start = system * inverse_frobenius
    root = split(start)
    inverse_root = plus_identity(1.5, -0.5 * start)
    factor = split(inverse_root)
    inverse_pair = factor
    root = split(product(root, factor))
    for number in range(1, ITERS):
        factor = split(plus_identity(1.5, -0.5 * product(root, inverse_pair)))
        if number < ITERS - 1:
            root = split(product(factor, root))
        inverse_root = product(inverse_pair, factor)
        inverse_pair = split(inverse_root)

    def row_product(row):
        pair = stack(*split(row))
        first = jnp.dot(pair, inverse_pair[0], preferred_element_type=F32)
        second = jnp.dot(pair, inverse_pair[1], preferred_element_type=F32)
        return first[0:1] + first[1:2] + second[0:1]

    mean_weight = row_product(row_product(projected)) * inverse_frobenius
    spread = math.sqrt(total - 1.0) / jnp.sqrt(frobenius)
    weights = (spread * inverse_root + mean_weight).astype(BF16)

    wait_block(main_recv, main_sems)
    cell_total = main_recv.shape[2]
    step = 2 * LANES
    for n in range(cell_total // step):
        at = slice(n * step, (n + 1) * step)
        prior = main_recv[:, :, at].reshape(total, step).astype(F32)
        mean = jnp.sum(prior, axis=0, keepdims=True) * (1.0 / total)
        update = jnp.dot(weights, (prior - mean).astype(BF16), preferred_element_type=F32)
        back_send[:, :, at] = (update + mean).astype(BF16).reshape(regions, members, step)

    for to in ring_order((1, -1, 2, -2, 3, -3, 4, 0)):
        block_copy(back_send, back_recv, back_sems, to, r).start()
    back_recv[r] = back_send[r]

    def finish_sends(d, carry):
        to = peer(d)
        cell_copy(to, r).wait_send()
        block_copy(main_send, main_recv, main_sems, to, r).wait_send()
        block_copy(obs_send, obs_recv, obs_sems, to, r).wait_send()
        return carry

    lax.fori_loop(1, regions, finish_sends, 0)
    finish_halo()

    def unpack_group(step, carry):
        group = lax.rem(first_group + step, groups)
        lanes = group_lanes(group)
        for t in range(4):
            tile = 4 * group + t

            @pl.when(tile != r)
            def _():
                block_copy(back_recv, back_recv, back_sems, tile, tile).wait_recv()

        for t in range(4):
            for s in range(8):
                shuffle[t, pl.ds(s, members, stride=8), :] = back_recv[
                    4 * group + t, :, s * LANES : (s + 1) * LANES
                ].astype(F32)
        for m in range(members):
            parts = swap_blocks([shuffle[t, m * 8 : m * 8 + 8, :] for t in range(4)])
            out[m, :, lanes] = jnp.concatenate(parts, axis=0).astype(BF16)
        return carry

    lax.fori_loop(0, groups, unpack_group, 0)

    def finish_back(d, carry):
        block_copy(back_send, back_recv, back_sems, peer(d), r).wait_send()
        return carry

    lax.fori_loop(1, regions, finish_back, 0)


def solution(mesh):
    regions = mesh.shape["region"]
    bands = mesh.shape["grp"]

    def shards(ensemble, obs_value, obs_prec, obs_index, obs_count):
        members, rows, columns = ensemble.shape
        slots = obs_index.shape[2]
        cells = rows * TILE
        return pl.pallas_call(
            functools.partial(kernel, regions, bands),
            out_shape=pltpu.VMEM(ensemble.shape, BF16),
            in_specs=[pl.BlockSpec(memory_space=pl.ANY)] * 5,
            out_specs=pl.BlockSpec(memory_space=pltpu.VMEM),
            scratch_shapes=[
                pltpu.VMEM((members, rows, columns + 2 * LANES), BF16),
                pltpu.VMEM((members, rows, columns + 2 * LANES), BF16),
                pltpu.VMEM((2, rows, 2 * LANES), BF16),
                pltpu.VMEM((2, rows, 2 * LANES), BF16),
                pltpu.VMEM((regions, 1, slots), jnp.int32),
                pltpu.VMEM((1, 1), jnp.int32),
                pltpu.VMEM((4, members * 8, LANES), F32),
                pltpu.VMEM((regions, members, cells), BF16),
                pltpu.VMEM((regions, members, cells), BF16),
                pltpu.VMEM((regions, members, slots), F32),
                pltpu.VMEM((regions, members, slots), BF16),
                pltpu.VMEM((regions, members, slots), BF16),
                pltpu.VMEM((regions, members, cells), BF16),
                pltpu.VMEM((regions, members, cells), BF16),
                pltpu.SemaphoreType.DMA((5,)),
                pltpu.SemaphoreType.DMA((2, regions // 2)),
                pltpu.SemaphoreType.DMA((2, 4)),
                pltpu.SemaphoreType.DMA((2, regions)),
                pltpu.SemaphoreType.DMA((2, regions)),
                pltpu.SemaphoreType.DMA((2, regions)),
                pltpu.SemaphoreType.DMA((2, regions)),
            ],
            compiler_params=pltpu.CompilerParams(
                collective_id=0, has_side_effects=True, vmem_limit_bytes=60 * 1024 * 1024
            ),
        )(ensemble, obs_value, obs_prec, obs_index, obs_count)

    placed = (
        P("region", "grp", None),
        P("grp", None),
        P("grp", None),
        P("grp", "region", None),
        P("grp", "region"),
    )
    return jax.shard_map(
        shards, mesh=mesh, in_specs=placed, out_specs=P("region", "grp", None), check_vma=False
    )
```
